512 devices in a mesh: expert: 2 (over x_hi), dp: 16 (over z), seq: 16 (over y, x_lo, core).
Axes of the slice: x: 4 (x_hi: 2, x_lo: 2; x = x_hi * 2 + x_lo), y: 4, z: 16, core: 2. Of those that a mesh axis runs over, the one named last changes fastest.
Arguments:
- queries: bfloat16 [32, 2048, 4096], P(('expert', 'dp'), 'seq'), may hold values from -6 to 6
- key_states: bfloat16 [32, 2048, 4096], P(('expert', 'dp'), 'seq'), may hold values from -6 to 6
- value_states: bfloat16 [32, 2048, 4096], P(('expert', 'dp'), 'seq'), may hold values from -6 to 6
- timesteps: int32 [32], P(('expert', 'dp')), may hold values from 0 to 999, as said below
- norm_gain: bfloat16 [2, 2, 4096], P('expert'), may hold values from 0.3984375 to 2.5
- cross_gain: bfloat16 [2, 4096], P('expert', 'seq'), may hold values from 0.3984375 to 2.5
- prompt_states: bfloat16 [2, 2, 2, 128, 4096], P('expert', None, None, None, 'seq'), may hold values from -52 to 52
- prompt_lengths: int32 [2], replicated, may hold values from 16 to 128, as said below
Outputs:
- guided: bfloat16 [32, 2048, 4096], P(('expert', 'dp'), 'seq')
The draws below stay inside these ranges and needn't reach their ends.
Inputs may be any that keep to these rules, and one draw needn't show every extreme that they name: `timesteps`: sample 0 has a timestep of at least 875, sample 1 one below it. `prompt_lengths`: one of the two equals 128.
All inputs are finite; a program needn't handle non-finite values.
Results may differ from the reference program's by a relative error of at most 0.035.
Values may be sent and summed in bfloat16 or wider, within the bound.
A program may use at most 128 MiB of HBM per device.

```python
import math
import jax
import jax.numpy as jnp
from jax import lax

HEADS = 32
HEAD_DIM = 128
TEXT_LEN = 128
BOUNDARY = 875
TIMESTEPS = 1000
EXPERT_GROUPS = 2
SAMPLES = 32
SEQ_LEN = 2048


def draw_queries(key, part):
    key = jax.random.fold_in(key, 11)
    full_shape = (SAMPLES, SEQ_LEN, HEADS * HEAD_DIM)
    drawn = jnp.clip(jax.random.normal(key, full_shape, jnp.float32), -6.0, 6.0)
    return drawn.astype(jnp.bfloat16)


def draw_key_states(key, part):
    key = jax.random.fold_in(key, 12)
    full_shape = (SAMPLES, SEQ_LEN, HEADS * HEAD_DIM)
    drawn = jnp.clip(jax.random.normal(key, full_shape, jnp.float32), -6.0, 6.0)
    return drawn.astype(jnp.bfloat16)


def draw_prompt_states(key, part):
    key = jax.random.fold_in(key, 13)
    key_first = jax.random.fold_in(key, 0)
    full_shape = (EXPERT_GROUPS, 2, 2, TEXT_LEN, HEADS * HEAD_DIM)
    drawn = jnp.clip(jax.random.normal(key_first, full_shape, jnp.float32), -6.0, 6.0)
    return drawn.astype(jnp.bfloat16)


def draw_timesteps(key, part):
    key = jax.random.fold_in(key, 14)
    key_first, key_second, key_third = jax.random.split(key, 3)
    steps_drawn = jax.random.randint(key_first, (SAMPLES,), 0, TIMESTEPS)
    high_step = jax.random.randint(key_second, (), BOUNDARY, TIMESTEPS)
    low_step = jax.random.randint(key_third, (), 0, BOUNDARY)
    return steps_drawn.at[0].set(high_step).at[1].set(low_step).astype(jnp.int32)


def draw_prompt_lengths(key, part):
    key = jax.random.fold_in(key, 15)
    key_first, key_second = jax.random.split(key)
    lengths_drawn = jax.random.randint(key_first, (2,), TEXT_LEN // 8, TEXT_LEN + 1)
    longest = jax.random.randint(key_second, (), 0, 2)
    return jnp.where(jnp.arange(2) == longest, TEXT_LEN, lengths_drawn).astype(jnp.int32)


def block_levels(stream_key, shape, cuts, least, top_value):
    def one(position, parts):
        draws = jax.random.uniform(jax.random.fold_in(jax.random.fold_in(stream_key, 6), position), (parts,), jnp.float32, least / len(cuts), top_value / len(cuts))
        return jnp.repeat(jnp.exp(draws), shape[position] // parts).reshape((-1,) + (1,) * (len(shape) - position - 1))

    level = one(*cuts[0])
    for cut in cuts[1:]:
        level = level * one(*cut)
    return level


def bell_draw(key, dims, width, reach, pieces=(), held_as=jnp.bfloat16):
    array = width * jax.random.normal(key, dims, jnp.float32)
    if pieces:
        array = array * block_levels(key, dims, pieces, -0.22, 0.18)
    return jnp.clip(array, -reach, reach).astype(held_as)


def setup_inputs(seed: int = 0) -> dict:
    key_of = jax.random.split(jax.random.key(seed), 9)
    queries = draw_queries(jax.random.fold_in(key_of[8], 71), 0)
    key_states = draw_key_states(jax.random.fold_in(key_of[8], 71), 0)
    value_states = bell_draw(key_of[2], (SAMPLES, SEQ_LEN, HEADS * HEAD_DIM), 1.0, 6.0, ((0, 32), (1, 16)))
    timesteps = draw_timesteps(jax.random.fold_in(key_of[8], 71), 0)
    norm_gain = jnp.clip(jnp.exp(math.log(2.5) - 1.8364954 * jax.random.uniform(key_of[4], (EXPERT_GROUPS, 2, HEADS * HEAD_DIM), jnp.float32) ** block_levels(key_of[4], (EXPERT_GROUPS, 2, HEADS * HEAD_DIM), ((0, 2),), -0.2, 0.2)), 0.3984375, 2.5).astype(jnp.bfloat16)
    cross_gain = jnp.clip(jnp.exp(math.log(2.5) - 1.8364954 * jax.random.uniform(key_of[5], (EXPERT_GROUPS, HEADS * HEAD_DIM), jnp.float32) ** block_levels(key_of[5], (EXPERT_GROUPS, HEADS * HEAD_DIM), ((0, 2), (1, 16)), -0.2, 0.2)), 0.3984375, 2.5).astype(jnp.bfloat16)
    prompt_states = draw_prompt_states(jax.random.fold_in(key_of[8], 71), 0)
    prompt_lengths = draw_prompt_lengths(jax.random.fold_in(key_of[8], 71), 0)
    return dict(queries=queries, key_states=key_states, value_states=value_states, timesteps=timesteps, norm_gain=norm_gain, cross_gain=cross_gain, prompt_states=prompt_states, prompt_lengths=prompt_lengths)


GUIDANCE = 5.0

def rms_scale(values, gain):
    mean_square = lax.optimization_barrier(jnp.mean(values * values, axis=-1, keepdims=True))
    return values * lax.rsqrt(mean_square + 1e-06) * gain.astype(jnp.float32)

def attend(query_rows, key_rows, value_rows, visible):
    scores = jnp.einsum('rhd,khd->hrk', query_rows.astype(jnp.float32), key_rows.astype(jnp.float32)) * HEAD_DIM ** (-0.5)
    if visible is not None:
        scores = jnp.where(visible, scores, -jnp.inf)
    row_peak = lax.optimization_barrier(jnp.max(scores, axis=-1, keepdims=True))
    weights = jnp.exp(scores - row_peak)
    probabilities = (weights / lax.optimization_barrier(jnp.sum(weights, axis=-1, keepdims=True))).astype(jnp.bfloat16)
    return jnp.einsum('hrk,khd->rhd', probabilities.astype(jnp.float32), value_rows.astype(jnp.float32))

def reference(queries, key_states, value_states, timesteps, norm_gain, cross_gain, prompt_states, prompt_lengths):
    visible = jnp.arange(TEXT_LEN)[None, :] < prompt_lengths[:, None]

    def one_sample(inputs):
        query_in, key_in, value_in, step_index = inputs
        expert_index = jnp.where(step_index >= BOUNDARY, 0, 1).astype(jnp.int32)
        gains = lax.dynamic_index_in_dim(norm_gain, expert_index, 0, keepdims=False)
        cross_scale = lax.dynamic_index_in_dim(cross_gain, expert_index, 0, keepdims=False)
        tables = lax.dynamic_index_in_dim(prompt_states, expert_index, 0, keepdims=False)
        query_normed = rms_scale(query_in.astype(jnp.float32), gains[0]).astype(jnp.bfloat16)
        key_normed = rms_scale(key_in.astype(jnp.float32), gains[1]).astype(jnp.bfloat16)
        shape_heads = (SEQ_LEN, HEADS, HEAD_DIM)
        self_out = attend(query_normed.reshape(shape_heads), key_normed.reshape(shape_heads), value_in.reshape(shape_heads), None).astype(jnp.bfloat16)
        cross_query = rms_scale(self_out.astype(jnp.float32), cross_scale.reshape(HEADS, HEAD_DIM)).astype(jnp.bfloat16)
        prompt_heads = tables.reshape(2, 2, TEXT_LEN, HEADS, HEAD_DIM)
        positive = attend(cross_query, prompt_heads[0, 0], prompt_heads[0, 1], visible[0][None, None, :])
        negative = attend(cross_query, prompt_heads[1, 0], prompt_heads[1, 1], visible[1][None, None, :])
        guided = self_out.astype(jnp.float32) + negative + GUIDANCE * (positive - negative)
        return guided.reshape(SEQ_LEN, HEADS * HEAD_DIM).astype(jnp.bfloat16)
    return lax.map(one_sample, (queries, key_states, value_states, timesteps))
```

```python
import functools
import math

import jax
import jax.numpy as jnp
from jax import lax
from jax.experimental import pallas as pl
from jax.experimental.pallas import tpu as pltpu
from jax.sharding import PartitionSpec as P

HEAD_DIM = 128
BOUNDARY = 875
GUIDANCE = 5.0
EPS = 1e-06
SCORE_SCALE = math.log2(math.e) / math.sqrt(HEAD_DIM)
MESH = pl.DeviceIdType.MESH
ROWS_OF_Y = 4
NT = (((1,), (1,)), ((), ()))


def place(me):
    return me // 4, (me // 2) % 2, me % 2


def source_of(me, i):
    y, x, core = place(me)
    chip = i // 2
    y, x, core = (y + chip // 2) % ROWS_OF_Y, (x + chip % 2) % 2, (core + i % 2) % 2
    return (y * 2 + x) * 2 + core


def target_of(me, i):
    y, x, core = place(me)
    chip = i // 2
    y, x, core = (y + ROWS_OF_Y - chip // 2) % ROWS_OF_Y, (x + chip % 2) % 2, (core + i % 2) % 2
    return (y * 2 + x) * 2 + core


def kernel(
    sizes,
    steps_ref, lengths_ref, q_ref, k_ref, v_ref, gain_ref, cross_gain_ref, prompt_ref,
    out_ref,
    q_rows, k_rows, gain_rows, cross_rows,
    q_got, k_got, v_got,
    k_normed, v_wide, out_blocks,
    scale_own, scale_got, k_scale, q_scale,
    gains, tables, cross_keys, cross_values,
    row_sems, q_sems, k_sems, v_sems, scale_sems, send_sems,
    out_sem, gain_sem, table_own_sem, piece_sem, table_sem,
):
    parts, groups, tok, cols = sizes
    expert = lax.axis_index("expert")
    dp = lax.axis_index("dp")
    me = lax.axis_index("seq")
    other = 1 - expert
    piece = tables.shape[1] // groups

    barrier = pltpu.get_barrier_semaphore()

    def greet_seq(i, carry):
        pl.semaphore_signal(barrier, 1, device_id={"seq": (me + i) % parts}, device_id_type=MESH)
        return carry

    def greet_dp(i, carry):
        pl.semaphore_signal(barrier, 1, device_id={"dp": (dp + i) % groups}, device_id_type=MESH)
        return carry

    lax.fori_loop(1, parts, greet_seq, 0)
    pl.semaphore_signal(barrier, 1, device_id={"expert": other}, device_id_type=MESH)
    lax.fori_loop(1, groups, greet_dp, 0)

    own_cols = pl.ds(pl.multiple_of(me * cols, cols), cols)
    local = [
        pltpu.make_async_copy(gain_ref, gain_rows, row_sems.at[0]),
        pltpu.make_async_copy(cross_gain_ref, cross_rows, row_sems.at[1]),
        pltpu.make_async_copy(k_ref, k_rows, row_sems.at[2]),
        pltpu.make_async_copy(q_ref, q_rows, row_sems.at[3]),
        pltpu.make_async_copy(prompt_ref, tables.at[0], table_own_sem),
        pltpu.make_async_copy(k_ref.at[:, own_cols], k_got.at[me], k_sems.at[me]),
        pltpu.make_async_copy(v_ref.at[:, own_cols], v_got.at[me], v_sems.at[me]),
        pltpu.make_async_copy(q_ref.at[:, own_cols], q_got.at[me], q_sems.at[me]),
    ]
    for copy in local:
        copy.start()
    v_wide[:, :, HEAD_DIM:] = jnp.ones((2, parts * tok, HEAD_DIM), jnp.bfloat16)

    pl.semaphore_wait(barrier, parts + groups - 1)

    def spread(src, got, sems, kind):
        def one(i, carry):
            d = target_of(me, i)
            theirs = pl.ds(pl.multiple_of(d * cols, cols), cols)
            pltpu.make_async_remote_copy(
                src_ref=src.at[:, theirs], dst_ref=got.at[me],
                send_sem=send_sems.at[kind], recv_sem=sems.at[me],
                device_id={"seq": d}, device_id_type=MESH,
            ).start()
            return carry

        lax.fori_loop(1, parts, one, 0)

    def await_bytes(ref, sem):
        pltpu.make_async_copy(ref, ref, sem).wait()

    spread(k_ref, k_got, k_sems, 0)

    mine = pl.ds(pl.multiple_of(dp * piece, piece), piece)
    fetch = pltpu.make_async_remote_copy(
        src_ref=prompt_ref.at[mine], dst_ref=tables.at[1, mine],
        send_sem=send_sems.at[5], recv_sem=piece_sem,
        device_id={"expert": other}, device_id_type=MESH,
    )
    fetch.start()

    local[0].wait()
    local[1].wait()
    gains[0, 0:2, :] = gain_rows[:, own_cols].astype(jnp.float32)
    gains[0, 2:3, :] = cross_rows[...].astype(jnp.float32)
    gains[0, 3:8, :] = jnp.zeros((5, cols), jnp.float32)
    swap = pltpu.make_async_remote_copy(
        src_ref=gains.at[0], dst_ref=gains.at[1],
        send_sem=send_sems.at[6], recv_sem=gain_sem,
        device_id={"expert": other}, device_id_type=MESH,
    )
    swap.start()

    def inverse_rms(rows):
        def add(c, total):
            part = rows[:, pl.ds(pl.multiple_of(c * 512, 512), 512)].astype(jnp.float32)
            part = part * part
            return total + (
                (part[:, :128] + part[:, 128:256]) + (part[:, 256:384] + part[:, 384:])
            )

        width = rows.shape[1]
        total = lax.fori_loop(0, width // 512, add, jnp.zeros((tok, 128), jnp.float32))
        mean = jnp.sum(jnp.transpose(total), axis=0, keepdims=True) / width
        return lax.rsqrt(mean + EPS)

    local[2].wait()
    scale_own[0:1, :] = inverse_rms(k_rows)
    local[3].wait()
    scale_own[1:2, :] = inverse_rms(q_rows)
    scale_own[2:8, :] = jnp.zeros((6, tok), jnp.float32)
    scale_got[me] = scale_own[...]

    def send_scale(i, carry):
        d = target_of(me, i)
        pltpu.make_async_remote_copy(
            src_ref=scale_own, dst_ref=scale_got.at[me],
            send_sem=send_sems.at[3], recv_sem=scale_sems.at[me],
            device_id={"seq": d}, device_id_type=MESH,
        ).start()
        return carry

    lax.fori_loop(1, parts, send_scale, 0)

    fetch.wait_recv()

    def pass_on(i, carry):
        pltpu.make_async_remote_copy(
            src_ref=tables.at[1, mine], dst_ref=tables.at[1, mine],
            send_sem=send_sems.at[7], recv_sem=table_sem,
            device_id={"dp": (dp + i) % groups}, device_id_type=MESH,
        ).start()
        return carry

    lax.fori_loop(1, groups, pass_on, 0)

    spread(v_ref, v_got, v_sems, 1)
    spread(q_ref, q_got, q_sems, 2)

    swap.wait_recv()

    def await_scale(i, carry):
        s = source_of(me, i)
        await_bytes(scale_got.at[s], scale_sems.at[s])
        return carry

    lax.fori_loop(1, parts, await_scale, 0)
    flipped = jnp.transpose(scale_got[...].reshape(parts * 8, tok))
    for s in range(parts):
        k_scale[s] = jnp.broadcast_to(flipped[:, 8 * s : 8 * s + 1], (tok, 128))
        q_scale[s] = jnp.broadcast_to(flipped[:, 8 * s + 1 : 8 * s + 2], (tok, 128))

    routed = jnp.where(steps_ref[0] >= BOUNDARY, 0, 1)
    choice = jnp.where(routed == expert, 0, 1)
    chosen = gains[choice]
    q_gain = chosen[0:1, :] * SCORE_SCALE
    k_gain = chosen[1:2, :]
    cross_gain = chosen[2:3, :] * SCORE_SCALE

    def take_keys(i, carry):
        s = source_of(me, i)
        await_bytes(k_got.at[s], k_sems.at[s])
        scale = k_scale[s]
        for h in range(2):
            lanes = slice(h * HEAD_DIM, (h + 1) * HEAD_DIM)
            normed = k_got[s, :, lanes].astype(jnp.float32) * scale * k_gain[:, lanes]
            k_normed[h, pl.ds(pl.multiple_of(s * tok, tok), tok), :] = normed.astype(jnp.bfloat16)
        return carry

    lax.fori_loop(0, parts, take_keys, 0)

    local[4].wait()
    fetch.wait_send()
    await_bytes(tables.at[1, pl.ds(0, piece * (groups - 1))], table_sem)
    for h in range(2):
        lanes = slice(h * HEAD_DIM, (h + 1) * HEAD_DIM)
        for b in range(2):
            rows = slice(b * 128, (b + 1) * 128)
            cross_keys[h, rows, :] = tables[choice, b * 256 : b * 256 + 128, lanes]
            cross_values[h, rows, :] = tables[choice, b * 256 + 128 : b * 256 + 256, lanes]

    def take_values(i, carry):
        s = source_of(me, i)
        await_bytes(v_got.at[s], v_sems.at[s])
        for h in range(2):
            lanes = slice(h * HEAD_DIM, (h + 1) * HEAD_DIM)
            v_wide[h, pl.ds(pl.multiple_of(s * tok, tok), tok), :HEAD_DIM] = v_got[s, :, lanes]
        return carry

    lax.fori_loop(0, parts, take_values, 0)

    position = lax.broadcasted_iota(jnp.int32, (2 * tok, 128), 1)
    visible = [position < lengths_ref[b] for b in range(2)]
    weight = (GUIDANCE, 1.0 - GUIDANCE)

    def attend(j, carry):
        s = (source_of(me, 2 * j) // 2) * 2
        for c in range(2):
            await_bytes(q_got.at[s + c], q_sems.at[s + c])
        pair = pl.ds(s, 2)
        scale = q_scale[pair].reshape(2 * tok, 128)
        for h in range(2):
            lanes = slice(h * HEAD_DIM, (h + 1) * HEAD_DIM)
            rows = q_got[pair, :, lanes].reshape(2 * tok, HEAD_DIM).astype(jnp.float32)
            query = (rows * scale * q_gain[:, lanes]).astype(jnp.bfloat16)
            scores = lax.dot_general(query, k_normed[h], NT, preferred_element_type=jnp.float32)
            peak = jnp.max(scores, axis=1, keepdims=True)
            weights = jnp.exp2(scores - peak).astype(jnp.bfloat16)
            sums = jnp.dot(weights, v_wide[h], preferred_element_type=jnp.float32)
            self_out = (sums[:, :HEAD_DIM] / sums[:, HEAD_DIM:]).astype(jnp.bfloat16)
            self_out = self_out.astype(jnp.float32)
            mean = jnp.mean(self_out * self_out, axis=1, keepdims=True)
            cross_query = self_out * lax.rsqrt(mean + EPS) * cross_gain[:, lanes]
            cross_scores = lax.dot_general(
                cross_query.astype(jnp.bfloat16), cross_keys[h], NT,
                preferred_element_type=jnp.float32,
            )
            shares = []
            for b in range(2):
                branch = jnp.where(
                    visible[b], cross_scores[:, b * 128 : (b + 1) * 128], -jnp.inf
                )
                branch = jnp.exp2(branch - jnp.max(branch, axis=1, keepdims=True))
                factor = weight[b] / jnp.sum(branch, axis=1, keepdims=True)
                shares.append((branch * factor).astype(jnp.bfloat16))
            guided = self_out + jnp.dot(
                jnp.concatenate(shares, axis=1), cross_values[h],
                preferred_element_type=jnp.float32,
            )
            out_blocks[pair, :, lanes] = guided.astype(jnp.bfloat16).reshape(2, tok, HEAD_DIM)
        for c in range(2):
            d = s + c

            @pl.when(d != me)
            def _():
                pltpu.make_async_remote_copy(
                    src_ref=out_blocks.at[d], dst_ref=out_ref.at[:, own_cols],
                    send_sem=send_sems.at[4], recv_sem=out_sem,
                    device_id={"seq": d}, device_id_type=MESH,
                ).start()

            @pl.when(d == me)
            def _():
                pltpu.make_async_copy(out_blocks.at[d], out_ref.at[:, own_cols], out_sem).start()

        return carry

    lax.fori_loop(0, parts // 2, attend, 0)

    swap.wait_send()
    some = pl.ds(0, parts - 1)
    await_bytes(k_got.at[some], send_sems.at[0])
    await_bytes(v_got.at[some], send_sems.at[1])
    await_bytes(q_got.at[some], send_sems.at[2])
    await_bytes(scale_got.at[some], send_sems.at[3])
    await_bytes(tables.at[1, pl.ds(0, piece * (groups - 1))], send_sems.at[7])
    await_bytes(out_blocks.at[some], send_sems.at[4])
    await_bytes(out_ref, out_sem)


def body(q, k, v, timesteps, norm_gain, cross_gain, prompts, lengths):
    parts, groups = lax.axis_size("seq"), lax.axis_size("dp")
    _, tok, width = q.shape
    cols = width // parts
    text = prompts.shape[3]
    bf16, f32 = jnp.bfloat16, jnp.float32
    hbm = pl.BlockSpec(memory_space=pltpu.HBM)
    smem = pl.BlockSpec(memory_space=pltpu.SMEM)
    dma = pltpu.SemaphoreType.DMA
    out = pl.pallas_call(
        functools.partial(kernel, (parts, groups, tok, cols)),
        out_shape=jax.ShapeDtypeStruct((tok, width), bf16),
        in_specs=[smem, smem] + [hbm] * 6,
        out_specs=hbm,
        scratch_shapes=[
            pltpu.VMEM((tok, width), bf16),
            pltpu.VMEM((tok, width), bf16),
            pltpu.VMEM((2, width), bf16),
            pltpu.VMEM((1, cols), bf16),
            pltpu.VMEM((parts, tok, cols), bf16),
            pltpu.VMEM((parts, tok, cols), bf16),
            pltpu.VMEM((parts, tok, cols), bf16),
            pltpu.VMEM((2, parts * tok, HEAD_DIM), bf16),
            pltpu.VMEM((2, parts * tok, 2 * HEAD_DIM), bf16),
            pltpu.VMEM((parts, tok, cols), bf16),
            pltpu.VMEM((8, tok), f32),
            pltpu.VMEM((parts, 8, tok), f32),
            pltpu.VMEM((parts, tok, 128), f32),
            pltpu.VMEM((parts, tok, 128), f32),
            pltpu.VMEM((2, 8, cols), f32),
            pltpu.VMEM((2, 4 * text, cols), bf16),
            pltpu.VMEM((2, 2 * text, HEAD_DIM), bf16),
            pltpu.VMEM((2, 2 * text, HEAD_DIM), bf16),
            dma((4,)),
            dma((parts,)),
            dma((parts,)),
            dma((parts,)),
            dma((parts,)),
            dma((8,)),
            dma,
            dma,
            dma,
            dma,
            dma,
        ],
        compiler_params=pltpu.CompilerParams(
            collective_id=0, has_side_effects=True, vmem_limit_bytes=63 * 2**20
        ),
        name="guided_attention",
    )(
        timesteps, lengths,
        q.reshape(tok, width), k.reshape(tok, width), v.reshape(tok, width),
        norm_gain.reshape(2, width), cross_gain, prompts.reshape(4 * text, cols),
    )
    return out[None]


def solution(mesh):
    placed = (
        P(("expert", "dp"), "seq", None),
        P(("expert", "dp"), "seq", None),
        P(("expert", "dp"), "seq", None),
        P(("expert", "dp")),
        P("expert", None, None),
        P("expert", "seq"),
        P("expert", None, None, None, "seq"),
        P(),
    )
    return jax.shard_map(
        body,
        mesh=mesh,
        in_specs=placed,
        out_specs=P(("expert", "dp"), "seq", None),
        check_vma=False,
    )
```

```python
import functools
import math

import jax
import jax.numpy as jnp
from jax import lax
from jax.experimental import pallas as pl
from jax.experimental.pallas import tpu as pltpu
from jax.sharding import PartitionSpec as P

HEAD_DIM = 128
BOUNDARY = 875
GUIDANCE = 5.0
EPS = 1e-06
SCORE_SCALE = math.log2(math.e) / math.sqrt(HEAD_DIM)
MESH = pl.DeviceIdType.MESH
ROWS_OF_Y = 4
NT = (((1,), (1,)), ((), ()))


def place(me):
    return me // 4, (me // 2) % 2, me % 2


def source_of(me, i):
    y, x, core = place(me)
    chip = i // 2
    y, x, core = (y + chip // 2) % ROWS_OF_Y, (x + chip % 2) % 2, (core + i % 2) % 2
    return (y * 2 + x) * 2 + core


def target_of(me, i):
    y, x, core = place(me)
    chip = i // 2
    y, x, core = (y + ROWS_OF_Y - chip // 2) % ROWS_OF_Y, (x + chip % 2) % 2, (core + i % 2) % 2
    return (y * 2 + x) * 2 + core


def kernel(
    sizes,
    steps_ref, lengths_ref, q_ref, k_ref, v_ref, gain_ref, cross_gain_ref, prompt_ref,
    out_ref,
    q_rows, k_rows, v_rows, gain_rows, cross_rows,
    q_sent, k_sent, v_sent,
    q_got, k_got, v_got,
    k_normed, v_wide, out_blocks, out_got,
    scale_own, scale_got, k_scale, q_scale,
    gains, tables, cross_keys, cross_values,
    row_sems, q_sems, k_sems, v_sems, scale_sems, send_sems,
    out_sem, gain_sem, table_own_sem, table_sem,
):
    parts, tok, cols = sizes
    expert = lax.axis_index("expert")
    me = lax.axis_index("seq")

    def across(d):
        return d + 2 - 4 * ((d // 2) % 2)

    routed = jnp.where(steps_ref[0] >= BOUNDARY, 0, 1)
    choice = jnp.where(routed == expert, 0, 1)

    def pick(here, there):
        return lax.select_n(choice == 1, here, there)

    partner = {"expert": 1 - expert, "seq": across(me)}

    barrier = pltpu.get_barrier_semaphore()

    def greet(i, carry):
        pl.semaphore_signal(barrier, 1, device_id={"seq": (me + i) % parts}, device_id_type=MESH)
        return carry

    lax.fori_loop(1, parts, greet, 0)
    pl.semaphore_signal(barrier, 1, device_id=partner, device_id_type=MESH)

    own_cols = pl.ds(pl.multiple_of(me * cols, cols), cols)
    local = [
        pltpu.make_async_copy(k_ref, k_rows, row_sems.at[0]),
        pltpu.make_async_copy(gain_ref, gain_rows, row_sems.at[1]),
        pltpu.make_async_copy(cross_gain_ref, cross_rows, row_sems.at[2]),
        pltpu.make_async_copy(q_ref, q_rows, row_sems.at[3]),
        pltpu.make_async_copy(v_ref, v_rows, row_sems.at[4]),
        pltpu.make_async_copy(prompt_ref, tables.at[0], table_own_sem),
    ]
    for copy in local:
        copy.start()

    def stage(rows, sent):
        def one(d, carry):
            here = pl.ds(pl.multiple_of(d * cols, cols), cols)
            there = pl.ds(pl.multiple_of(across(d) * cols, cols), cols)
            sent[d] = pick(rows[:, here], rows[:, there])
            return carry

        lax.fori_loop(0, parts, one, 0)

    def spread(sent, got, sems, kind):
        def one(i, carry):
            d = target_of(me, i)
            pltpu.make_async_remote_copy(
                src_ref=sent.at[d], dst_ref=got.at[me],
                send_sem=send_sems.at[kind], recv_sem=sems.at[me],
                device_id={"seq": d}, device_id_type=MESH,
            ).start()
            return carry

        lax.fori_loop(1, parts, one, 0)

    def await_bytes(ref, sem):
        pltpu.make_async_copy(ref, ref, sem).wait()

    local[0].wait()
    stage(k_rows, k_sent)
    pl.semaphore_wait(barrier, parts)
    spread(k_sent, k_got, k_sems, 0)

    local[1].wait()
    local[2].wait()
    gains[0, 0:2, :] = gain_rows[:, own_cols].astype(jnp.float32)
    gains[0, 2:3, :] = cross_rows[...].astype(jnp.float32)
    gains[0, 3:8, :] = jnp.zeros((5, cols), jnp.float32)
    swap = pltpu.make_async_remote_copy(
        src_ref=gains.at[0], dst_ref=gains.at[1],
        send_sem=send_sems.at[6], recv_sem=gain_sem,
        device_id=partner, device_id_type=MESH,
    )
    swap.start()
    fetch = pltpu.make_async_remote_copy(
        src_ref=prompt_ref, dst_ref=tables.at[1],
        send_sem=send_sems.at[5], recv_sem=table_sem,
        device_id=partner, device_id_type=MESH,
    )
    fetch.start()

    def inverse_rms(rows):
        def add(c, total):
            part = rows[:, pl.ds(pl.multiple_of(c * 512, 512), 512)].astype(jnp.float32)
            part = part * part
            return total + (
                (part[:, :128] + part[:, 128:256]) + (part[:, 256:384] + part[:, 384:])
            )

        width = rows.shape[1]
        total = lax.fori_loop(0, width // 512, add, jnp.zeros((tok, 128), jnp.float32))
        mean = jnp.sum(jnp.transpose(total), axis=0, keepdims=True) / width
        return lax.rsqrt(mean + EPS)

    scale_own[0:1, :] = inverse_rms(k_rows)
    local[3].wait()
    scale_own[1:2, :] = inverse_rms(q_rows)
    scale_own[2:8, :] = jnp.zeros((6, tok), jnp.float32)
    scale_got[me] = scale_own[...]

    def send_scale(i, carry):
        d = target_of(me, i)
        pltpu.make_async_remote_copy(
            src_ref=scale_own, dst_ref=scale_got.at[me],
            send_sem=send_sems.at[3], recv_sem=scale_sems.at[me],
            device_id={"seq": d}, device_id_type=MESH,
        ).start()
        return carry

    lax.fori_loop(1, parts, send_scale, 0)

    local[4].wait()
    stage(v_rows, v_sent)
    spread(v_sent, v_got, v_sems, 1)
    stage(q_rows, q_sent)
    spread(q_sent, q_got, q_sems, 2)
    k_got[me] = k_sent[me]
    v_got[me] = v_sent[me]
    q_got[me] = q_sent[me]
    v_wide[:, :, HEAD_DIM:] = jnp.ones((2, parts * tok, HEAD_DIM), jnp.bfloat16)

    swap.wait_recv()

    def await_scale(i, carry):
        s = source_of(me, i)
        await_bytes(scale_got.at[s], scale_sems.at[s])
        return carry

    lax.fori_loop(1, parts, await_scale, 0)
    flipped = jnp.transpose(scale_got[...].reshape(parts * 8, tok))
    for s in range(parts):
        k_scale[s] = jnp.broadcast_to(flipped[:, 8 * s : 8 * s + 1], (tok, 128))
        q_scale[s] = jnp.broadcast_to(flipped[:, 8 * s + 1 : 8 * s + 2], (tok, 128))

    chosen = gains[choice]
    q_gain = chosen[0:1, :] * SCORE_SCALE
    k_gain = chosen[1:2, :]
    cross_gain = chosen[2:3, :] * SCORE_SCALE

    def take_keys(i, carry):
        s = source_of(me, i)

        @pl.when(i > 0)
        def _():
            await_bytes(k_got.at[s], k_sems.at[s])

        scale = k_scale[s]
        for h in range(2):
            lanes = slice(h * HEAD_DIM, (h + 1) * HEAD_DIM)
            normed = k_got[s, :, lanes].astype(jnp.float32) * scale * k_gain[:, lanes]
            k_normed[h, pl.ds(pl.multiple_of(s * tok, tok), tok), :] = normed.astype(jnp.bfloat16)
        return carry

    lax.fori_loop(0, parts, take_keys, 0)

    local[5].wait()
    fetch.wait_recv()
    for h in range(2):
        lanes = slice(h * HEAD_DIM, (h + 1) * HEAD_DIM)
        for b in range(2):
            rows = slice(b * 128, (b + 1) * 128)
            cross_keys[h, rows, :] = tables[choice, b * 256 : b * 256 + 128, lanes]
            cross_values[h, rows, :] = tables[choice, b * 256 + 128 : b * 256 + 256, lanes]

    def take_values(i, carry):
        s = source_of(me, i)

        @pl.when(i > 0)
        def _():
            await_bytes(v_got.at[s], v_sems.at[s])

        for h in range(2):
            lanes = slice(h * HEAD_DIM, (h + 1) * HEAD_DIM)
            v_wide[h, pl.ds(pl.multiple_of(s * tok, tok), tok), :HEAD_DIM] = v_got[s, :, lanes]
        return carry

    lax.fori_loop(0, parts, take_values, 0)

    position = lax.broadcasted_iota(jnp.int32, (2 * tok, 128), 1)
    visible = [position < lengths_ref[b] for b in range(2)]
    weight = (GUIDANCE, 1.0 - GUIDANCE)

    def self_scores(pair, h):
        lanes = slice(h * HEAD_DIM, (h + 1) * HEAD_DIM)
        rows = q_got[pair, :, lanes].reshape(2 * tok, HEAD_DIM).astype(jnp.float32)
        scale = q_scale[pair].reshape(2 * tok, 128)
        query = (rows * scale * q_gain[:, lanes]).astype(jnp.bfloat16)
        return lax.dot_general(query, k_normed[h], NT, preferred_element_type=jnp.float32)

    def softmax_weights(scores):
        peak = jnp.max(scores, axis=1, keepdims=True)
        return jnp.exp2(scores - peak).astype(jnp.bfloat16)

    def self_values(weights, h):
        sums = jnp.dot(weights, v_wide[h], preferred_element_type=jnp.float32)
        self_out = (sums[:, :HEAD_DIM] / sums[:, HEAD_DIM:]).astype(jnp.bfloat16)
        return self_out.astype(jnp.float32)

    def cross_scores(self_out, h):
        lanes = slice(h * HEAD_DIM, (h + 1) * HEAD_DIM)
        mean = jnp.mean(self_out * self_out, axis=1, keepdims=True)
        query = self_out * lax.rsqrt(mean + EPS) * cross_gain[:, lanes]
        return lax.dot_general(
            query.astype(jnp.bfloat16), cross_keys[h], NT, preferred_element_type=jnp.float32
        )

    def cross_weights(scores):
        shares = []
        for b in range(2):
            branch = jnp.where(visible[b], scores[:, b * 128 : (b + 1) * 128], -jnp.inf)
            branch = jnp.exp2(branch - jnp.max(branch, axis=1, keepdims=True))
            factor = weight[b] / jnp.sum(branch, axis=1, keepdims=True)
            shares.append((branch * factor).astype(jnp.bfloat16))
        return jnp.concatenate(shares, axis=1)

    def attend(j, carry):
        s = (source_of(me, 2 * j) // 2) * 2
        for c in range(2):

            @pl.when(s + c != me)
            def _():
                await_bytes(q_got.at[s + c], q_sems.at[s + c])

        pair = pl.ds(s, 2)
        heads = range(2)
        scores = [self_scores(pair, h) for h in heads]
        weights = [softmax_weights(scores[h]) for h in heads]
        self_out = [self_values(weights[h], h) for h in heads]
        scores = [cross_scores(self_out[h], h) for h in heads]
        shares = [cross_weights(scores[h]) for h in heads]
        for h in heads:
            lanes = slice(h * HEAD_DIM, (h + 1) * HEAD_DIM)
            guided = self_out[h] + jnp.dot(
                shares[h], cross_values[h], preferred_element_type=jnp.float32
            )
            out_blocks[pair, :, lanes] = guided.astype(jnp.bfloat16).reshape(2, tok, HEAD_DIM)
        for c in range(2):
            d = s + c

            @pl.when(d != me)
            def _():
                pltpu.make_async_remote_copy(
                    src_ref=out_blocks.at[d], dst_ref=out_got.at[me],
                    send_sem=send_sems.at[4], recv_sem=out_sem,
                    device_id={"seq": d}, device_id_type=MESH,
                ).start()

            @pl.when(d == me)
            def _():
                out_got[me] = out_blocks[me]

        return carry

    lax.fori_loop(0, parts // 2, attend, 0)

    swap.wait_send()
    fetch.wait_send()
    some = pl.ds(0, parts - 1)
    await_bytes(k_got.at[some], send_sems.at[0])
    await_bytes(v_got.at[some], send_sems.at[1])
    await_bytes(q_got.at[some], send_sems.at[2])
    await_bytes(scale_got.at[some], send_sems.at[3])
    await_bytes(out_blocks.at[some], send_sems.at[4])
    await_bytes(out_got.at[some], out_sem)

    for d in range(parts):
        out_ref[:, d * cols : (d + 1) * cols] = pick(out_got[d], out_got[across(d)])


def body(q, k, v, timesteps, norm_gain, cross_gain, prompts, lengths):
    parts = lax.axis_size("seq")
    _, tok, width = q.shape
    cols = width // parts
    text = prompts.shape[3]
    bf16, f32 = jnp.bfloat16, jnp.float32
    hbm = pl.BlockSpec(memory_space=pltpu.HBM)
    smem = pl.BlockSpec(memory_space=pltpu.SMEM)
    dma = pltpu.SemaphoreType.DMA
    blocks = pltpu.VMEM((parts, tok, cols), bf16)
    out = pl.pallas_call(
        functools.partial(kernel, (parts, tok, cols)),
        out_shape=jax.ShapeDtypeStruct((tok, width), bf16),
        in_specs=[smem, smem] + [hbm] * 6,
        out_specs=pl.BlockSpec(memory_space=pltpu.VMEM),
        scratch_shapes=[
            pltpu.VMEM((tok, width), bf16),
            pltpu.VMEM((tok, width), bf16),
            pltpu.VMEM((tok, width), bf16),
            pltpu.VMEM((2, width), bf16),
            pltpu.VMEM((1, cols), bf16),
            blocks, blocks, blocks,
            blocks, blocks, blocks,
            pltpu.VMEM((2, parts * tok, HEAD_DIM), bf16),
            pltpu.VMEM((2, parts * tok, 2 * HEAD_DIM), bf16),
            blocks, blocks,
            pltpu.VMEM((8, tok), f32),
            pltpu.VMEM((parts, 8, tok), f32),
            pltpu.VMEM((parts, tok, 128), f32),
            pltpu.VMEM((parts, tok, 128), f32),
            pltpu.VMEM((2, 8, cols), f32),
            pltpu.VMEM((2, 4 * text, cols), bf16),
            pltpu.VMEM((2, 2 * text, HEAD_DIM), bf16),
            pltpu.VMEM((2, 2 * text, HEAD_DIM), bf16),
            dma((5,)),
            dma((parts,)),
            dma((parts,)),
            dma((parts,)),
            dma((parts,)),
            dma((7,)),
            dma,
            dma,
            dma,
            dma,
        ],
        compiler_params=pltpu.CompilerParams(
            collective_id=0, has_side_effects=True, vmem_limit_bytes=63 * 2**20
        ),
        name="guided_attention",
    )(
        timesteps, lengths,
        q.reshape(tok, width), k.reshape(tok, width), v.reshape(tok, width),
        norm_gain.reshape(2, width), cross_gain, prompts.reshape(4 * text, cols),
    )
    return out[None]


def solution(mesh):
    placed = (
        P(("expert", "dp"), "seq", None),
        P(("expert", "dp"), "seq", None),
        P(("expert", "dp"), "seq", None),
        P(("expert", "dp")),
        P("expert", None, None),
        P("expert", "seq"),
        P("expert", None, None, None, "seq"),
        P(),
    )
    return jax.shard_map(
        body,
        mesh=mesh,
        in_specs=placed,
        out_specs=P(("expert", "dp"), "seq", None),
        check_vma=False,
    )
```

```python
import functools
import math

import jax
import jax.numpy as jnp
from jax import lax
from jax.experimental import pallas as pl
from jax.experimental.pallas import tpu as pltpu
from jax.sharding import PartitionSpec as P

HEAD_DIM = 128
BOUNDARY = 875
GUIDANCE = 5.0
EPS = 1e-06
SCORE_SCALE = math.log2(math.e) / math.sqrt(HEAD_DIM)
MESH = pl.DeviceIdType.MESH
ROWS_OF_Y = 4
NT = (((1,), (1,)), ((), ()))


CHIPS = (5, 3, 7, 4, 1, 2, 6, 0)
CHIP_CODE = sum(chip * 8**i for i, chip in enumerate(CHIPS))


def over_chips(count, visit):
    def step(_, code):
        visit(code % 8)
        return code // 8

    lax.fori_loop(0, count, step, jnp.int32(CHIP_CODE))


def shifted(me, y_steps, x_steps, core_steps):
    y, x, core = me // 4, (me // 2) % 2, me % 2
    y, x, core = (y + y_steps) % ROWS_OF_Y, (x + x_steps) % 2, (core + core_steps) % 2
    return (y * 2 + x) * 2 + core


def source_of(me, chip, core_steps):
    return shifted(me, chip // 2, chip % 2, core_steps)


def target_of(me, chip, core_steps):
    return shifted(me, ROWS_OF_Y - chip // 2, chip % 2, core_steps)


def across(d):
    return d + 2 - 4 * ((d // 2) % 2)


def choice_of(steps_ref):
    routed = jnp.where(steps_ref[0] >= BOUNDARY, 0, 1)
    return jnp.where(routed == lax.axis_index("expert"), 0, 1)


def kernel(
    sizes,
    steps_ref, lengths_ref, q_ref, k_ref, v_ref, gain_ref, cross_gain_ref, prompt_ref,
    out_ref,
    q_rows, k_rows, v_rows, gain_rows, cross_rows,
    q_sent, k_sent, v_sent,
    q_got, k_got, v_got,
    k_normed, v_wide, out_blocks,
    scale_own, scale_got, k_scale, q_scale,
    gains, tables, cross_keys, cross_values,
    row_sems, q_sems, k_sems, v_sems, scale_sems, send_sems,
    out_sem, gain_sem, table_own_sem, table_sem, late_sem, late_partner_sem,
):
    parts, tok, cols = sizes
    expert = lax.axis_index("expert")
    me = lax.axis_index("seq")

    choice = choice_of(steps_ref)

    def pick(here, there):
        return lax.select_n(choice == 1, here, there)

    partner = {"expert": 1 - expert, "seq": across(me)}

    barrier = pltpu.get_barrier_semaphore()

    def signal_group(sem):
        def one(i, carry):
            pl.semaphore_signal(sem, 1, device_id={"seq": (me + i) % parts}, device_id_type=MESH)
            return carry

        lax.fori_loop(1, parts, one, 0)

    scale_got[...] = jnp.zeros_like(scale_got)

    @pl.when(me != 0)
    def _():
        signal_group(barrier)
        pl.semaphore_signal(barrier, 1, device_id=partner, device_id_type=MESH)

    own_cols = pl.ds(pl.multiple_of(me * cols, cols), cols)
    local = [
        pltpu.make_async_copy(k_ref, k_rows, row_sems.at[0]),
        pltpu.make_async_copy(gain_ref, gain_rows, row_sems.at[1]),
        pltpu.make_async_copy(cross_gain_ref, cross_rows, row_sems.at[2]),
        pltpu.make_async_copy(q_ref, q_rows, row_sems.at[3]),
        pltpu.make_async_copy(v_ref, v_rows, row_sems.at[4]),
        pltpu.make_async_copy(prompt_ref, tables.at[0], table_own_sem),
    ]
    for copy in local:
        copy.start()

    def stage(rows, sent):
        def one(d, carry):
            here = pl.ds(pl.multiple_of(d * cols, cols), cols)
            there = pl.ds(pl.multiple_of(across(d) * cols, cols), cols)
            sent[d] = pick(rows[:, here], rows[:, there])
            return carry

        lax.fori_loop(0, parts, one, 0)

    def to_group(send):
        def chip(c):
            for core in range(2):
                send(target_of(me, c, core))

        over_chips(parts // 2 - 1, chip)
        send(shifted(me, 0, 0, 1))

    def sender(sent, got, sems, kind):
        def send(d):
            pltpu.make_async_remote_copy(
                src_ref=sent.at[d], dst_ref=got.at[me],
                send_sem=send_sems.at[kind], recv_sem=sems.at[me],
                device_id={"seq": d}, device_id_type=MESH,
            ).start()

        return send

    def send_scale(d):
        pltpu.make_async_remote_copy(
            src_ref=scale_own.at[0:2], dst_ref=scale_got.at[me, 0:2],
            send_sem=send_sems.at[3], recv_sem=scale_sems.at[me],
            device_id={"seq": d}, device_id_type=MESH,
        ).start()

    def but_first(send):
        def guarded(d):
            @pl.when(d != 0)
            def _():
                send(d)

        return guarded

    def await_bytes(ref, sem):
        pltpu.make_async_copy(ref, ref, sem).wait()

    local[0].wait()
    stage(k_rows, k_sent)

    @pl.when(me == 0)
    def _():
        pl.semaphore_wait(barrier, parts)
        signal_group(late_sem)
        pl.semaphore_signal(late_partner_sem, 1, device_id=partner, device_id_type=MESH)

    @pl.when(me == 2)
    def _():
        pl.semaphore_wait(barrier, parts - 2)

    @pl.when((me != 0) & (me != 2))
    def _():
        pl.semaphore_wait(barrier, parts - 1)

    send_keys = sender(k_sent, k_got, k_sems, 0)
    to_group(but_first(send_keys))

    def inverse_rms(rows):
        def add(c, total):
            part = rows[:, pl.ds(pl.multiple_of(c * 512, 512), 512)].astype(jnp.float32)
            part = part * part
            return total + (
                (part[:, :128] + part[:, 128:256]) + (part[:, 256:384] + part[:, 384:])
            )

        width = rows.shape[1]
        total = lax.fori_loop(0, width // 512, add, jnp.zeros((tok, 128), jnp.float32))
        mean = jnp.sum(jnp.transpose(total), axis=0, keepdims=True) / width
        return lax.rsqrt(mean + EPS)

    scale_own[0:1, :] = inverse_rms(k_rows)
    local[3].wait()
    scale_own[1:2, :] = inverse_rms(q_rows)
    scale_own[2:8, :] = jnp.zeros((6, tok), jnp.float32)
    scale_got[me] = scale_own[...]

    to_group(but_first(send_scale))

    local[1].wait()
    local[2].wait()
    gains[0, 0:2, :] = gain_rows[:, own_cols].astype(jnp.float32)
    gains[0, 2:3, :] = cross_rows[...].astype(jnp.float32)
    gains[0, 3:8, :] = jnp.zeros((5, cols), jnp.float32)
    swap = pltpu.make_async_remote_copy(
        src_ref=gains.at[0], dst_ref=gains.at[1],
        send_sem=send_sems.at[6], recv_sem=gain_sem,
        device_id=partner, device_id_type=MESH,
    )
    fetch = pltpu.make_async_remote_copy(
        src_ref=prompt_ref, dst_ref=tables.at[1],
        send_sem=send_sems.at[5], recv_sem=table_sem,
        device_id=partner, device_id_type=MESH,
    )
    local[4].wait()
    stage(v_rows, v_sent)
    stage(q_rows, q_sent)

    @pl.when(me != 0)
    def _():
        pl.semaphore_wait(late_sem, 1)
        send_keys(0)
        send_scale(0)

    @pl.when(me == 2)
    def _():
        pl.semaphore_wait(late_partner_sem, 1)

    swap.start()
    fetch.start()
    to_group(sender(v_sent, v_got, v_sems, 1))
    to_group(sender(q_sent, q_got, q_sems, 2))
    k_got[me] = k_sent[me]
    v_got[me] = v_sent[me]
    q_got[me] = q_sent[me]
    v_wide[:, :, HEAD_DIM:] = jnp.ones((2, parts * tok, HEAD_DIM), jnp.bfloat16)

    swap.wait_recv()

    def from_group(take):
        def chip(c):
            for core in range(2):
                take(source_of(me, c, core))

        over_chips(parts // 2, chip)

    def await_scale(s):
        @pl.when(s != me)
        def _():
            await_bytes(scale_got.at[s, 0:2], scale_sems.at[s])

    from_group(await_scale)
    flipped = jnp.transpose(scale_got[...].reshape(parts * 8, tok))
    for s in range(parts):
        k_scale[s] = jnp.broadcast_to(flipped[:, 8 * s : 8 * s + 1], (tok, 128))
        q_scale[s] = jnp.broadcast_to(flipped[:, 8 * s + 1 : 8 * s + 2], (tok, 128))

    chosen = gains[choice]
    q_gain = chosen[0:1, :] * SCORE_SCALE
    k_gain = chosen[1:2, :]
    cross_gain = chosen[2:3, :] * SCORE_SCALE

    def take_keys(s):
        @pl.when(s != me)
        def _():
            await_bytes(k_got.at[s], k_sems.at[s])

        scale = k_scale[s]
        for h in range(2):
            lanes = slice(h * HEAD_DIM, (h + 1) * HEAD_DIM)
            normed = k_got[s, :, lanes].astype(jnp.float32) * scale * k_gain[:, lanes]
            k_normed[h, pl.ds(pl.multiple_of(s * tok, tok), tok), :] = normed.astype(jnp.bfloat16)

    from_group(take_keys)

    local[5].wait()
    fetch.wait_recv()
    for h in range(2):
        lanes = slice(h * HEAD_DIM, (h + 1) * HEAD_DIM)
        for b in range(2):
            rows = slice(b * 128, (b + 1) * 128)
            cross_keys[h, rows, :] = tables[choice, b * 256 : b * 256 + 128, lanes]
            cross_values[h, rows, :] = tables[choice, b * 256 + 128 : b * 256 + 256, lanes]

    def take_values(s):
        @pl.when(s != me)
        def _():
            await_bytes(v_got.at[s], v_sems.at[s])

        for h in range(2):
            lanes = slice(h * HEAD_DIM, (h + 1) * HEAD_DIM)
            v_wide[h, pl.ds(pl.multiple_of(s * tok, tok), tok), :HEAD_DIM] = v_got[s, :, lanes]

    from_group(take_values)

    position = lax.broadcasted_iota(jnp.int32, (2 * tok, 128), 1)
    visible = [position < lengths_ref[b] for b in range(2)]
    weight = (GUIDANCE, 1.0 - GUIDANCE)

    def self_scores(pair, h):
        lanes = slice(h * HEAD_DIM, (h + 1) * HEAD_DIM)
        rows = q_got[pair, :, lanes].reshape(2 * tok, HEAD_DIM).astype(jnp.float32)
        scale = q_scale[pair].reshape(2 * tok, 128)
        query = (rows * scale * q_gain[:, lanes]).astype(jnp.bfloat16)
        return lax.dot_general(query, k_normed[h], NT, preferred_element_type=jnp.float32)

    def softmax_weights(scores):
        peak = jnp.max(scores, axis=1, keepdims=True)
        return jnp.exp2(scores - peak).astype(jnp.bfloat16)

    def self_values(weights, h):
        sums = jnp.dot(weights, v_wide[h], preferred_element_type=jnp.float32)
        self_out = (sums[:, :HEAD_DIM] / sums[:, HEAD_DIM:]).astype(jnp.bfloat16)
        return self_out.astype(jnp.float32)

    def cross_scores(self_out, h):
        lanes = slice(h * HEAD_DIM, (h + 1) * HEAD_DIM)
        mean = jnp.mean(self_out * self_out, axis=1, keepdims=True)
        query = self_out * lax.rsqrt(mean + EPS) * cross_gain[:, lanes]
        return lax.dot_general(
            query.astype(jnp.bfloat16), cross_keys[h], NT, preferred_element_type=jnp.float32
        )

    def cross_weights(scores):
        shares = []
        for b in range(2):
            branch = jnp.where(visible[b], scores[:, b * 128 : (b + 1) * 128], -jnp.inf)
            branch = jnp.exp2(branch - jnp.max(branch, axis=1, keepdims=True))
            factor = weight[b] / jnp.sum(branch, axis=1, keepdims=True)
            shares.append((branch * factor).astype(jnp.bfloat16))
        return jnp.concatenate(shares, axis=1)

    def attend(c):
        s = (source_of(me, c, 0) // 2) * 2
        for c in range(2):

            @pl.when(s + c != me)
            def _():
                await_bytes(q_got.at[s + c], q_sems.at[s + c])

        pair = pl.ds(s, 2)
        heads = range(2)
        scores = [self_scores(pair, h) for h in heads]
        weights = [softmax_weights(scores[h]) for h in heads]
        self_out = [self_values(weights[h], h) for h in heads]
        scores = [cross_scores(self_out[h], h) for h in heads]
        shares = [cross_weights(scores[h]) for h in heads]
        for h in heads:
            lanes = slice(h * HEAD_DIM, (h + 1) * HEAD_DIM)
            guided = self_out[h] + jnp.dot(
                shares[h], cross_values[h], preferred_element_type=jnp.float32
            )
            out_blocks[pair, :, lanes] = guided.astype(jnp.bfloat16).reshape(2, tok, HEAD_DIM)
        for c in range(2):
            d = s + c

            @pl.when(d != me)
            def _():
                pltpu.make_async_remote_copy(
                    src_ref=out_blocks.at[d], dst_ref=out_ref.at[me],
                    send_sem=send_sems.at[4], recv_sem=out_sem,
                    device_id={"seq": d}, device_id_type=MESH,
                ).start()

            @pl.when(d == me)
            def _():
                pltpu.make_async_copy(out_blocks.at[me], out_ref.at[me], out_sem).start()

    over_chips(parts // 2, attend)

    swap.wait_send()
    fetch.wait_send()
    some = pl.ds(0, parts - 1)
    await_bytes(k_got.at[some], send_sems.at[0])
    await_bytes(v_got.at[some], send_sems.at[1])
    await_bytes(q_got.at[some], send_sems.at[2])
    await_bytes(scale_got.at[some, 0:2], send_sems.at[3])
    await_bytes(out_blocks.at[some], send_sems.at[4])
    await_bytes(out_ref, out_sem)


def arrange(steps_ref, got_ref, out_ref, rows, in_sems, out_sems):
    parts, _, cols = got_ref.shape
    choice = choice_of(steps_ref)
    loads, stores = [], []
    for d in range(parts):
        worker = d + choice * (across(d) - d)
        lanes = slice(d * cols, (d + 1) * cols)
        loads.append(pltpu.make_async_copy(got_ref.at[worker], rows.at[d], in_sems.at[d]))
        stores.append(pltpu.make_async_copy(rows.at[d], out_ref.at[:, lanes], out_sems.at[d]))
    for load in loads:
        load.start()
    for load, store in zip(loads, stores):
        load.wait()
        store.start()
    for store in stores:
        store.wait()


def body(q, k, v, timesteps, norm_gain, cross_gain, prompts, lengths):
    parts = lax.axis_size("seq")
    _, tok, width = q.shape
    cols = width // parts
    text = prompts.shape[3]
    bf16, f32 = jnp.bfloat16, jnp.float32
    hbm = pl.BlockSpec(memory_space=pltpu.HBM)
    smem = pl.BlockSpec(memory_space=pltpu.SMEM)
    dma = pltpu.SemaphoreType.DMA
    blocks = pltpu.VMEM((parts, tok, cols), bf16)
    got = pl.pallas_call(
        functools.partial(kernel, (parts, tok, cols)),
        out_shape=jax.ShapeDtypeStruct((parts, tok, cols), bf16),
        in_specs=[smem, smem] + [hbm] * 6,
        out_specs=hbm,
        scratch_shapes=[
            pltpu.VMEM((tok, width), bf16),
            pltpu.VMEM((tok, width), bf16),
            pltpu.VMEM((tok, width), bf16),
            pltpu.VMEM((2, width), bf16),
            pltpu.VMEM((1, cols), bf16),
            blocks, blocks, blocks,
            blocks, blocks, blocks,
            pltpu.VMEM((2, parts * tok, HEAD_DIM), bf16),
            pltpu.VMEM((2, parts * tok, 2 * HEAD_DIM), bf16),
            blocks,
            pltpu.VMEM((8, tok), f32),
            pltpu.VMEM((parts, 8, tok), f32),
            pltpu.VMEM((parts, tok, 128), f32),
            pltpu.VMEM((parts, tok, 128), f32),
            pltpu.VMEM((2, 8, cols), f32),
            pltpu.VMEM((2, 4 * text, cols), bf16),
            pltpu.VMEM((2, 2 * text, HEAD_DIM), bf16),
            pltpu.VMEM((2, 2 * text, HEAD_DIM), bf16),
            dma((5,)),
            dma((parts,)),
            dma((parts,)),
            dma((parts,)),
            dma((parts,)),
            dma((7,)),
            dma,
            dma,
            dma,
            dma,
            pltpu.SemaphoreType.REGULAR,
            pltpu.SemaphoreType.REGULAR,
        ],
        compiler_params=pltpu.CompilerParams(
            collective_id=0, has_side_effects=True, vmem_limit_bytes=63 * 2**20
        ),
        name="guided_attention",
    )(
        timesteps, lengths,
        q.reshape(tok, width), k.reshape(tok, width), v.reshape(tok, width),
        norm_gain.reshape(2, width), cross_gain, prompts.reshape(4 * text, cols),
    )
    out = pl.pallas_call(
        arrange,
        out_shape=jax.ShapeDtypeStruct((tok, width), bf16),
        in_specs=[smem, hbm],
        out_specs=hbm,
        scratch_shapes=[blocks, dma((parts,)), dma((parts,))],
        compiler_params=pltpu.CompilerParams(vmem_limit_bytes=63 * 2**20),
        name="arrange",
    )(timesteps, got)
    return out[None]


def solution(mesh):
    placed = (
        P(("expert", "dp"), "seq", None),
        P(("expert", "dp"), "seq", None),
        P(("expert", "dp"), "seq", None),
        P(("expert", "dp")),
        P("expert", None, None),
        P("expert", "seq"),
        P("expert", None, None, None, "seq"),
        P(),
    )
    return jax.shard_map(
        body,
        mesh=mesh,
        in_specs=placed,
        out_specs=P(("expert", "dp"), "seq", None),
        check_vma=False,
    )
```

```python
import functools
import math

import jax
import jax.numpy as jnp
from jax import lax
from jax.experimental import pallas as pl
from jax.experimental.pallas import tpu as pltpu
from jax.sharding import PartitionSpec as P

HEAD_DIM = 128
BOUNDARY = 875
GUIDANCE = 5.0
EPS = 1e-06
SCORE_SCALE = math.log2(math.e) / math.sqrt(HEAD_DIM)
MESH = pl.DeviceIdType.MESH
ROWS_OF_Y = 4
NT = (((1,), (1,)), ((), ()))


CHIPS = (5, 3, 7, 4, 1, 2, 6, 0)
CHIP_CODE = sum(chip * 8**i for i, chip in enumerate(CHIPS))


def over_chips(count, visit, at_once=1):
    def step(_, code):
        visit(*(code // 8**i % 8 for i in range(at_once)))
        return code // 8**at_once

    lax.fori_loop(0, count // at_once, step, jnp.int32(CHIP_CODE))


def shifted(me, y_steps, x_steps, core_steps):
    y, x, core = me // 4, (me // 2) % 2, me % 2
    y, x, core = (y + y_steps) % ROWS_OF_Y, (x + x_steps) % 2, (core + core_steps) % 2
    return (y * 2 + x) * 2 + core


def source_of(me, chip, core_steps):
    return shifted(me, chip // 2, chip % 2, core_steps)


def target_of(me, chip, core_steps):
    return shifted(me, ROWS_OF_Y - chip // 2, chip % 2, core_steps)


def across(d):
    return d + 2 - 4 * ((d // 2) % 2)


def choice_of(steps_ref):
    routed = jnp.where(steps_ref[0] >= BOUNDARY, 0, 1)
    return jnp.where(routed == lax.axis_index("expert"), 0, 1)


def kernel(
    sizes,
    steps_ref, length_ref, q_ref, k_ref, v_ref, gain_ref, cross_gain_ref, prompt_ref,
    out_ref,
    lengths_ref, q_rows, k_rows, v_rows, gain_rows, cross_rows,
    q_sent, k_sent, v_sent,
    q_got, k_got, v_got,
    k_normed, v_wide, out_blocks,
    scale_own, scale_got, k_scale, q_scale,
    gains, tables, cross_keys, cross_values,
    row_sems, q_sems, k_sems, v_sems, scale_sems, send_sems,
    out_sem, gain_sem, table_own_sem, table_sem, late_sem, late_partner_sem,
):
    parts, tok, cols = sizes
    expert = lax.axis_index("expert")
    me = lax.axis_index("seq")

    choice = choice_of(steps_ref)

    def pick(here, there):
        return lax.select_n(choice == 1, here, there)

    partner = {"expert": 1 - expert, "seq": across(me)}

    barrier = pltpu.get_barrier_semaphore()

    def signal_group(sem):
        def one(i, carry):
            pl.semaphore_signal(sem, 1, device_id={"seq": (me + i) % parts}, device_id_type=MESH)
            return carry

        lax.fori_loop(1, parts, one, 0)

    scale_got[...] = jnp.zeros_like(scale_got)

    @pl.when(me != 0)
    def _():
        signal_group(barrier)
        pl.semaphore_signal(barrier, 1, device_id=partner, device_id_type=MESH)

    own_cols = pl.ds(pl.multiple_of(me * cols, cols), cols)
    local = [
        pltpu.make_async_copy(k_ref, k_rows, row_sems.at[0]),
        pltpu.make_async_copy(gain_ref, gain_rows, row_sems.at[1]),
        pltpu.make_async_copy(cross_gain_ref, cross_rows, row_sems.at[2]),
        pltpu.make_async_copy(q_ref, q_rows, row_sems.at[3]),
        pltpu.make_async_copy(v_ref, v_rows, row_sems.at[4]),
        pltpu.make_async_copy(prompt_ref, tables.at[0], table_own_sem),
        pltpu.make_async_copy(length_ref, lengths_ref, row_sems.at[5]),
    ]
    for copy in local:
        copy.start()

    def stage(rows, sent):
        def one(d, carry):
            here = pl.ds(pl.multiple_of(d * cols, cols), cols)
            there = pl.ds(pl.multiple_of(across(d) * cols, cols), cols)
            sent[d] = pick(rows[:, here], rows[:, there])
            return carry

        lax.fori_loop(0, parts, one, 0)

    def to_group(send):
        def chip(c):
            for core in range(2):
                send(target_of(me, c, core))

        over_chips(parts // 2 - 1, chip)
        send(shifted(me, 0, 0, 1))

    def sender(sent, got, sems, kind):
        def send(d):
            pltpu.make_async_remote_copy(
                src_ref=sent.at[d], dst_ref=got.at[me],
                send_sem=send_sems.at[kind], recv_sem=sems.at[me],
                device_id={"seq": d}, device_id_type=MESH,
            ).start()

        return send

    def send_scale(d):
        pltpu.make_async_remote_copy(
            src_ref=scale_own.at[0:2], dst_ref=scale_got.at[me, 0:2],
            send_sem=send_sems.at[3], recv_sem=scale_sems.at[me],
            device_id={"seq": d}, device_id_type=MESH,
        ).start()

    def but_first(send):
        def guarded(d):
            @pl.when(d != 0)
            def _():
                send(d)

        return guarded

    def await_bytes(ref, sem):
        pltpu.make_async_copy(ref, ref, sem).wait()

    local[0].wait()
    stage(k_rows, k_sent)

    @pl.when(me == 0)
    def _():
        pl.semaphore_wait(barrier, parts)
        signal_group(late_sem)
        pl.semaphore_signal(late_partner_sem, 1, device_id=partner, device_id_type=MESH)

    @pl.when(me == 2)
    def _():
        pl.semaphore_wait(barrier, parts - 2)

    @pl.when((me != 0) & (me != 2))
    def _():
        pl.semaphore_wait(barrier, parts - 1)

    send_keys = sender(k_sent, k_got, k_sems, 0)
    to_group(but_first(send_keys))

    def inverse_rms(rows):
        def add(c, total):
            part = rows[:, pl.ds(pl.multiple_of(c * 512, 512), 512)].astype(jnp.float32)
            part = part * part
            return total + (
                (part[:, :128] + part[:, 128:256]) + (part[:, 256:384] + part[:, 384:])
            )

        width = rows.shape[1]
        total = lax.fori_loop(0, width // 512, add, jnp.zeros((tok, 128), jnp.float32))
        mean = jnp.sum(jnp.transpose(total), axis=0, keepdims=True) / width
        return lax.rsqrt(mean + EPS)

    scale_own[0:1, :] = inverse_rms(k_rows)
    local[3].wait()
    scale_own[1:2, :] = inverse_rms(q_rows)
    scale_own[2:8, :] = jnp.zeros((6, tok), jnp.float32)
    scale_got[me] = scale_own[...]

    to_group(but_first(send_scale))

    local[1].wait()
    local[2].wait()
    gains[0, 0:2, :] = gain_rows[:, own_cols].astype(jnp.float32)
    gains[0, 2:3, :] = cross_rows[...].astype(jnp.float32)
    gains[0, 3:8, :] = jnp.zeros((5, cols), jnp.float32)
    swap = pltpu.make_async_remote_copy(
        src_ref=gains.at[0], dst_ref=gains.at[1],
        send_sem=send_sems.at[6], recv_sem=gain_sem,
        device_id=partner, device_id_type=MESH,
    )
    fetch = pltpu.make_async_remote_copy(
        src_ref=prompt_ref, dst_ref=tables.at[1],
        send_sem=send_sems.at[5], recv_sem=table_sem,
        device_id=partner, device_id_type=MESH,
    )
    local[4].wait()
    stage(v_rows, v_sent)
    stage(q_rows, q_sent)

    @pl.when(me != 0)
    def _():
        pl.semaphore_wait(late_sem, 1)
        send_keys(0)
        send_scale(0)

    @pl.when(me == 2)
    def _():
        pl.semaphore_wait(late_partner_sem, 1)

    swap.start()
    fetch.start()
    to_group(sender(v_sent, v_got, v_sems, 1))
    to_group(sender(q_sent, q_got, q_sems, 2))
    k_got[me] = k_sent[me]
    v_got[me] = v_sent[me]
    q_got[me] = q_sent[me]
    v_wide[:, :, HEAD_DIM:] = jnp.ones((2, parts * tok, HEAD_DIM), jnp.bfloat16)

    swap.wait_recv()

    def from_group(take):
        def chip(c):
            for core in range(2):
                take(source_of(me, c, core))

        over_chips(parts // 2, chip)

    def await_scale(s):
        @pl.when(s != me)
        def _():
            await_bytes(scale_got.at[s, 0:2], scale_sems.at[s])

    from_group(await_scale)
    flipped = jnp.transpose(scale_got[...].reshape(parts * 8, tok))
    for s in range(parts):
        k_scale[s] = jnp.broadcast_to(flipped[:, 8 * s : 8 * s + 1], (tok, 128))
        q_scale[s] = jnp.broadcast_to(flipped[:, 8 * s + 1 : 8 * s + 2], (tok, 128))

    chosen = gains[choice]
    q_gain = chosen[0:1, :] * SCORE_SCALE
    k_gain = chosen[1:2, :]
    cross_gain = chosen[2:3, :] * SCORE_SCALE

    def take_keys(s):
        @pl.when(s != me)
        def _():
            await_bytes(k_got.at[s], k_sems.at[s])

        scale = k_scale[s]
        for h in range(2):
            lanes = slice(h * HEAD_DIM, (h + 1) * HEAD_DIM)
            normed = k_got[s, :, lanes].astype(jnp.float32) * scale * k_gain[:, lanes]
            k_normed[h, pl.ds(pl.multiple_of(s * tok, tok), tok), :] = normed.astype(jnp.bfloat16)

    from_group(take_keys)

    local[5].wait()
    local[6].wait()
    fetch.wait_recv()
    for h in range(2):
        lanes = slice(h * HEAD_DIM, (h + 1) * HEAD_DIM)
        for b in range(2):
            rows = slice(b * 128, (b + 1) * 128)
            cross_keys[h, rows, :] = tables[choice, b * 256 : b * 256 + 128, lanes]
            cross_values[h, rows, :] = tables[choice, b * 256 + 128 : b * 256 + 256, lanes]

    def take_values(s):
        @pl.when(s != me)
        def _():
            await_bytes(v_got.at[s], v_sems.at[s])

        for h in range(2):
            lanes = slice(h * HEAD_DIM, (h + 1) * HEAD_DIM)
            v_wide[h, pl.ds(pl.multiple_of(s * tok, tok), tok), :HEAD_DIM] = v_got[s, :, lanes]

    from_group(take_values)

    position = lax.broadcasted_iota(jnp.int32, (4 * tok, 128), 1)
    visible = [position < lengths_ref[b] for b in range(2)]
    weight = (GUIDANCE, 1.0 - GUIDANCE)

    def self_scores(blocks, h):
        lanes = slice(h * HEAD_DIM, (h + 1) * HEAD_DIM)
        query = jnp.concatenate(
            [
                (q_got[d, :, lanes].astype(jnp.float32) * q_scale[d] * q_gain[:, lanes]).astype(
                    jnp.bfloat16
                )
                for d in blocks
            ],
            axis=0,
        )
        return lax.dot_general(query, k_normed[h], NT, preferred_element_type=jnp.float32)

    def softmax_weights(scores):
        peak = jnp.max(scores, axis=1, keepdims=True)
        return jnp.exp2(scores - peak).astype(jnp.bfloat16)

    def self_values(weights, h):
        sums = jnp.dot(weights, v_wide[h], preferred_element_type=jnp.float32)
        self_out = (sums[:, :HEAD_DIM] / sums[:, HEAD_DIM:]).astype(jnp.bfloat16)
        return self_out.astype(jnp.float32)

    def cross_scores(self_out, h):
        lanes = slice(h * HEAD_DIM, (h + 1) * HEAD_DIM)
        mean = jnp.mean(self_out * self_out, axis=1, keepdims=True)
        query = self_out * lax.rsqrt(mean + EPS) * cross_gain[:, lanes]
        return lax.dot_general(
            query.astype(jnp.bfloat16), cross_keys[h], NT, preferred_element_type=jnp.float32
        )

    def cross_weights(scores):
        shares = []
        for b in range(2):
            branch = jnp.where(visible[b], scores[:, b * 128 : (b + 1) * 128], -jnp.inf)
            branch = jnp.exp2(branch - jnp.max(branch, axis=1, keepdims=True))
            factor = weight[b] / jnp.sum(branch, axis=1, keepdims=True)
            shares.append((branch * factor).astype(jnp.bfloat16))
        return jnp.concatenate(shares, axis=1)

    def attend(*chips):
        blocks = []
        for c in chips:
            first = (source_of(me, c, 0) // 2) * 2
            blocks += [first, first + 1]
        for d in blocks:

            @pl.when(d != me)
            def _():
                await_bytes(q_got.at[d], q_sems.at[d])

        heads = range(2)
        scores = [self_scores(blocks, h) for h in heads]
        weights = [softmax_weights(scores[h]) for h in heads]
        self_out = [self_values(weights[h], h) for h in heads]
        scores = [cross_scores(self_out[h], h) for h in heads]
        shares = [cross_weights(scores[h]) for h in heads]
        for h in heads:
            lanes = slice(h * HEAD_DIM, (h + 1) * HEAD_DIM)
            guided = self_out[h] + jnp.dot(
                shares[h], cross_values[h], preferred_element_type=jnp.float32
            )
            guided = guided.astype(jnp.bfloat16)
            for i, d in enumerate(blocks):
                out_blocks[d, :, lanes] = guided[i * tok : (i + 1) * tok]
        for d in blocks:

            @pl.when(d != me)
            def _():
                pltpu.make_async_remote_copy(
                    src_ref=out_blocks.at[d], dst_ref=out_ref.at[me],
                    send_sem=send_sems.at[4], recv_sem=out_sem,
                    device_id={"seq": d}, device_id_type=MESH,
                ).start()

            @pl.when(d == me)
            def _():
                pltpu.make_async_copy(out_blocks.at[me], out_ref.at[me], out_sem).start()

    over_chips(parts // 2, attend, at_once=2)

    swap.wait_send()
    fetch.wait_send()
    some = pl.ds(0, parts - 1)
    await_bytes(k_got.at[some], send_sems.at[0])
    await_bytes(v_got.at[some], send_sems.at[1])
    await_bytes(q_got.at[some], send_sems.at[2])
    await_bytes(scale_got.at[some, 0:2], send_sems.at[3])
    await_bytes(out_blocks.at[some], send_sems.at[4])
    await_bytes(out_ref, out_sem)


def arrange(steps_ref, got_ref, out_ref, sems):
    parts, _, cols = got_ref.shape
    choice = choice_of(steps_ref)
    copies = []
    for d in range(parts):
        worker = d + choice * (across(d) - d)
        lanes = slice(d * cols, (d + 1) * cols)
        copies.append(pltpu.make_async_copy(got_ref.at[worker], out_ref.at[:, lanes], sems.at[d]))
    for copy in copies:
        copy.start()
    for copy in copies:
        copy.wait()


def body(q, k, v, timesteps, norm_gain, cross_gain, prompts, lengths):
    parts = lax.axis_size("seq")
    _, tok, width = q.shape
    cols = width // parts
    text = prompts.shape[3]
    bf16, f32 = jnp.bfloat16, jnp.float32
    hbm = pl.BlockSpec(memory_space=pltpu.HBM)
    vmem = pl.BlockSpec(memory_space=pltpu.VMEM)
    smem = pl.BlockSpec(memory_space=pltpu.SMEM)
    dma = pltpu.SemaphoreType.DMA
    blocks = pltpu.VMEM((parts, tok, cols), bf16)
    got = pl.pallas_call(
        functools.partial(kernel, (parts, tok, cols)),
        out_shape=blocks,
        in_specs=[smem] + [hbm] * 7,
        out_specs=vmem,
        scratch_shapes=[
            pltpu.SMEM((2,), jnp.int32),
            pltpu.VMEM((tok, width), bf16),
            pltpu.VMEM((tok, width), bf16),
            pltpu.VMEM((tok, width), bf16),
            pltpu.VMEM((2, width), bf16),
            pltpu.VMEM((1, cols), bf16),
            blocks, blocks, blocks,
            blocks, blocks, blocks,
            pltpu.VMEM((2, parts * tok, HEAD_DIM), bf16),
            pltpu.VMEM((2, parts * tok, 2 * HEAD_DIM), bf16),
            blocks,
            pltpu.VMEM((8, tok), f32),
            pltpu.VMEM((parts, 8, tok), f32),
            pltpu.VMEM((parts, tok, 128), f32),
            pltpu.VMEM((parts, tok, 128), f32),
            pltpu.VMEM((2, 8, cols), f32),
            pltpu.VMEM((2, 4 * text, cols), bf16),
            pltpu.VMEM((2, 2 * text, HEAD_DIM), bf16),
            pltpu.VMEM((2, 2 * text, HEAD_DIM), bf16),
            dma((6,)),
            dma((parts,)),
            dma((parts,)),
            dma((parts,)),
            dma((parts,)),
            dma((7,)),
            dma,
            dma,
            dma,
            dma,
            pltpu.SemaphoreType.REGULAR,
            pltpu.SemaphoreType.REGULAR,
        ],
        compiler_params=pltpu.CompilerParams(
            collective_id=0, has_side_effects=True, vmem_limit_bytes=44 * 2**20
        ),
        name="guided_attention",
    )(
        timesteps,
        *(
            pltpu.with_memory_space_constraint(x, pltpu.HBM)
            for x in (
                lengths,
                q.reshape(tok, width), k.reshape(tok, width), v.reshape(tok, width),
                norm_gain.reshape(2, width), cross_gain, prompts.reshape(4 * text, cols),
            )
        ),
    )
    out = pl.pallas_call(
        arrange,
        out_shape=jax.ShapeDtypeStruct((tok, width), bf16),
        in_specs=[smem, vmem],
        out_specs=hbm,
        scratch_shapes=[dma((parts,))],
        compiler_params=pltpu.CompilerParams(vmem_limit_bytes=8 * 2**20),
        name="arrange",
    )(timesteps, got)
    return out[None]


def solution(mesh):
    placed = (
        P(("expert", "dp"), "seq", None),
        P(("expert", "dp"), "seq", None),
        P(("expert", "dp"), "seq", None),
        P(("expert", "dp")),
        P("expert", None, None),
        P("expert", "seq"),
        P("expert", None, None, None, "seq"),
        P(),
    )
    return jax.shard_map(
        body,
        mesh=mesh,
        in_specs=placed,
        out_specs=P(("expert", "dp"), "seq", None),
        check_vma=False,
    )
```

```python
import functools
import math

import jax
import jax.numpy as jnp
from jax import lax
from jax.experimental import pallas as pl
from jax.experimental.pallas import tpu as pltpu
from jax.sharding import PartitionSpec as P

HEAD_DIM = 128
BOUNDARY = 875
GUIDANCE = 5.0
EPS = 1e-06
SCORE_SCALE = math.log2(math.e) / math.sqrt(HEAD_DIM)
MESH = pl.DeviceIdType.MESH
ROWS_OF_Y = 4
NT = (((1,), (1,)), ((), ()))


CHIPS = (5, 3, 7, 4, 1, 2, 6, 0)
CHIP_CODE = sum(chip * 8**i for i, chip in enumerate(CHIPS))


def over_chips(count, visit, at_once=1):
    def step(_, code):
        visit(*(code // 8**i % 8 for i in range(at_once)))
        return code // 8**at_once

    lax.fori_loop(0, count // at_once, step, jnp.int32(CHIP_CODE))


def shifted(me, y_steps, x_steps, core_steps):
    y, x, core = me // 4, (me // 2) % 2, me % 2
    y, x, core = (y + y_steps) % ROWS_OF_Y, (x + x_steps) % 2, (core + core_steps) % 2
    return (y * 2 + x) * 2 + core


def source_of(me, chip, core_steps):
    return shifted(me, chip // 2, chip % 2, core_steps)


def target_of(me, chip, core_steps):
    return shifted(me, ROWS_OF_Y - chip // 2, chip % 2, core_steps)


def across(d):
    return d + 2 - 4 * ((d // 2) % 2)


def choice_of(steps_ref):
    routed = jnp.where(steps_ref[0] >= BOUNDARY, 0, 1)
    return jnp.where(routed == lax.axis_index("expert"), 0, 1)


def kernel(
    sizes,
    steps_ref, length_ref, q_ref, k_ref, v_ref, gain_ref, cross_gain_ref, prompt_ref,
    out_ref,
    lengths_ref, q_rows, k_rows, v_rows, gain_rows, cross_rows,
    q_sent, k_sent, v_sent,
    q_got, k_got, v_got,
    k_normed, v_wide, out_blocks,
    scale_own, scale_got, k_scale, q_scale,
    gains, tables, cross_keys, cross_values,
    row_sems, q_sems, k_sems, v_sems, scale_sems, send_sems,
    out_sem, gain_sem, table_own_sem, table_sem, late_sem, late_partner_sem,
):
    parts, tok, cols = sizes
    expert = lax.axis_index("expert")
    me = lax.axis_index("seq")

    choice = choice_of(steps_ref)

    def pick(here, there):
        return lax.select_n(choice == 1, here, there)

    partner = {"expert": 1 - expert, "seq": across(me)}

    barrier = pltpu.get_barrier_semaphore()

    def signal_group(sem):
        def one(i, carry):
            pl.semaphore_signal(sem, 1, device_id={"seq": (me + i) % parts}, device_id_type=MESH)
            return carry

        lax.fori_loop(1, parts, one, 0)

    scale_got[...] = jnp.zeros_like(scale_got)

    @pl.when(me != 0)
    def _():
        signal_group(barrier)
        pl.semaphore_signal(barrier, 1, device_id=partner, device_id_type=MESH)

    own_cols = pl.ds(pl.multiple_of(me * cols, cols), cols)
    local = [
        pltpu.make_async_copy(k_ref, k_rows, row_sems.at[0]),
        pltpu.make_async_copy(gain_ref, gain_rows, row_sems.at[1]),
        pltpu.make_async_copy(cross_gain_ref, cross_rows, row_sems.at[2]),
        pltpu.make_async_copy(q_ref, q_rows, row_sems.at[3]),
        pltpu.make_async_copy(v_ref, v_rows, row_sems.at[4]),
        pltpu.make_async_copy(prompt_ref, tables.at[0], table_own_sem),
        pltpu.make_async_copy(length_ref, lengths_ref, row_sems.at[5]),
    ]
    for copy in local:
        copy.start()

    def stage(rows, sent):
        def one(d, carry):
            here = pl.ds(pl.multiple_of(d * cols, cols), cols)
            there = pl.ds(pl.multiple_of(across(d) * cols, cols), cols)
            both = pick(rows[:, here], rows[:, there])
            for h in range(2):
                sent[h, d] = both[:, h * HEAD_DIM : (h + 1) * HEAD_DIM]
            return carry

        lax.fori_loop(0, parts, one, 0)

    def to_group(send):
        def chip(c):
            for core in range(2):
                send(target_of(me, c, core))

        over_chips(parts // 2 - 1, chip)
        send(shifted(me, 0, 0, 1))

    def sender(sent, got, sems, kind, h):
        def send(d):
            pltpu.make_async_remote_copy(
                src_ref=sent.at[h, d], dst_ref=got.at[h, me],
                send_sem=send_sems.at[2 * kind + h], recv_sem=sems.at[h, me],
                device_id={"seq": d}, device_id_type=MESH,
            ).start()

        return send

    def send_scale(d):
        pltpu.make_async_remote_copy(
            src_ref=scale_own.at[0:2], dst_ref=scale_got.at[me, 0:2],
            send_sem=send_sems.at[8], recv_sem=scale_sems.at[me],
            device_id={"seq": d}, device_id_type=MESH,
        ).start()

    def but_first(send):
        def guarded(d):
            @pl.when(d != 0)
            def _():
                send(d)

        return guarded

    def await_bytes(ref, sem):
        pltpu.make_async_copy(ref, ref, sem).wait()

    local[0].wait()
    stage(k_rows, k_sent)

    @pl.when(me == 0)
    def _():
        pl.semaphore_wait(barrier, parts)
        signal_group(late_sem)
        pl.semaphore_signal(late_partner_sem, 1, device_id=partner, device_id_type=MESH)

    @pl.when(me == 2)
    def _():
        pl.semaphore_wait(barrier, parts - 2)

    @pl.when((me != 0) & (me != 2))
    def _():
        pl.semaphore_wait(barrier, parts - 1)

    send_keys = sender(k_sent, k_got, k_sems, 0, 0)
    to_group(but_first(send_keys))

    def inverse_rms(rows):
        def add(c, total):
            part = rows[:, pl.ds(pl.multiple_of(c * 512, 512), 512)].astype(jnp.float32)
            part = part * part
            return total + (
                (part[:, :128] + part[:, 128:256]) + (part[:, 256:384] + part[:, 384:])
            )

        width = rows.shape[1]
        total = lax.fori_loop(0, width // 512, add, jnp.zeros((tok, 128), jnp.float32))
        mean = jnp.sum(jnp.transpose(total), axis=0, keepdims=True) / width
        return lax.rsqrt(mean + EPS)

    scale_own[0:1, :] = inverse_rms(k_rows)
    local[3].wait()
    scale_own[1:2, :] = inverse_rms(q_rows)
    scale_own[2:8, :] = jnp.zeros((6, tok), jnp.float32)
    scale_got[me] = scale_own[...]

    to_group(but_first(send_scale))

    local[1].wait()
    local[2].wait()
    gains[0, 0:2, :] = gain_rows[:, own_cols].astype(jnp.float32)
    gains[0, 2:3, :] = cross_rows[...].astype(jnp.float32)
    gains[0, 3:8, :] = jnp.zeros((5, cols), jnp.float32)
    swap = pltpu.make_async_remote_copy(
        src_ref=gains.at[0], dst_ref=gains.at[1],
        send_sem=send_sems.at[9], recv_sem=gain_sem,
        device_id=partner, device_id_type=MESH,
    )
    fetch = pltpu.make_async_remote_copy(
        src_ref=prompt_ref, dst_ref=tables.at[1],
        send_sem=send_sems.at[10], recv_sem=table_sem,
        device_id=partner, device_id_type=MESH,
    )

    @pl.when(me == 2)
    def _():
        pl.semaphore_wait(late_partner_sem, 1)

    swap.start()
    fetch.start()
    local[4].wait()
    stage(v_rows, v_sent)
    send_values = sender(v_sent, v_got, v_sems, 1, 0)
    to_group(but_first(send_values))
    stage(q_rows, q_sent)

    @pl.when(me != 0)
    def _():
        pl.semaphore_wait(late_sem, 1)
        send_keys(0)
        send_scale(0)
        send_values(0)

    to_group(sender(q_sent, q_got, q_sems, 2, 0))
    to_group(sender(k_sent, k_got, k_sems, 0, 1))
    to_group(sender(v_sent, v_got, v_sems, 1, 1))
    to_group(sender(q_sent, q_got, q_sems, 2, 1))
    for h in range(2):
        k_got[h, me] = k_sent[h, me]
        v_got[h, me] = v_sent[h, me]
        q_got[h, me] = q_sent[h, me]
    v_wide[:, :, HEAD_DIM:] = jnp.ones((2, parts * tok, HEAD_DIM), jnp.bfloat16)

    swap.wait_recv()

    def from_group(take):
        def chip(c):
            for core in range(2):
                take(source_of(me, c, core))

        over_chips(parts // 2, chip)

    def await_scale(s):
        @pl.when(s != me)
        def _():
            await_bytes(scale_got.at[s, 0:2], scale_sems.at[s])

    from_group(await_scale)
    flipped = jnp.transpose(scale_got[...].reshape(parts * 8, tok))
    for s in range(parts):
        k_scale[s] = jnp.broadcast_to(flipped[:, 8 * s : 8 * s + 1], (tok, 128))
        q_scale[s] = jnp.broadcast_to(flipped[:, 8 * s + 1 : 8 * s + 2], (tok, 128))

    chosen = gains[choice]
    q_gain = chosen[0:1, :] * SCORE_SCALE
    k_gain = chosen[1:2, :]
    cross_gain = chosen[2:3, :] * SCORE_SCALE

    def take_keys(s, h):
        @pl.when(s != me)
        def _():
            await_bytes(k_got.at[h, s], k_sems.at[h, s])

        lanes = slice(h * HEAD_DIM, (h + 1) * HEAD_DIM)
        normed = k_got[h, s].astype(jnp.float32) * k_scale[s] * k_gain[:, lanes]
        k_normed[h, pl.ds(pl.multiple_of(s * tok, tok), tok), :] = normed.astype(jnp.bfloat16)

    def take_values(s, h):
        @pl.when(s != me)
        def _():
            await_bytes(v_got.at[h, s], v_sems.at[h, s])

        v_wide[h, pl.ds(pl.multiple_of(s * tok, tok), tok), :HEAD_DIM] = v_got[h, s]

    def take(h):
        from_group(lambda s: take_keys(s, h))
        from_group(lambda s: take_values(s, h))

    take(0)

    local[5].wait()
    local[6].wait()
    fetch.wait_recv()
    for h in range(2):
        lanes = slice(h * HEAD_DIM, (h + 1) * HEAD_DIM)
        for b in range(2):
            rows = slice(b * 128, (b + 1) * 128)
            cross_keys[h, rows, :] = tables[choice, b * 256 : b * 256 + 128, lanes]
            cross_values[h, rows, :] = tables[choice, b * 256 + 128 : b * 256 + 256, lanes]

    position = lax.broadcasted_iota(jnp.int32, (4 * tok, 128), 1)
    visible = [position < lengths_ref[b] for b in range(2)]
    weight = (GUIDANCE, 1.0 - GUIDANCE)

    def self_scores(blocks, h):
        lanes = slice(h * HEAD_DIM, (h + 1) * HEAD_DIM)
        query = jnp.concatenate(
            [
                (q_got[h, d].astype(jnp.float32) * q_scale[d] * q_gain[:, lanes]).astype(
                    jnp.bfloat16
                )
                for d in blocks
            ],
            axis=0,
        )
        return lax.dot_general(query, k_normed[h], NT, preferred_element_type=jnp.float32)

    def softmax_weights(scores):
        peak = jnp.max(scores, axis=1, keepdims=True)
        return jnp.exp2(scores - peak).astype(jnp.bfloat16)

    def self_values(weights, h):
        sums = jnp.dot(weights, v_wide[h], preferred_element_type=jnp.float32)
        self_out = (sums[:, :HEAD_DIM] / sums[:, HEAD_DIM:]).astype(jnp.bfloat16)
        return self_out.astype(jnp.float32)

    def cross_scores(self_out, h):
        lanes = slice(h * HEAD_DIM, (h + 1) * HEAD_DIM)
        mean = jnp.mean(self_out * self_out, axis=1, keepdims=True)
        query = self_out * lax.rsqrt(mean + EPS) * cross_gain[:, lanes]
        return lax.dot_general(
            query.astype(jnp.bfloat16), cross_keys[h], NT, preferred_element_type=jnp.float32
        )

    def cross_weights(scores):
        shares = []
        for b in range(2):
            branch = jnp.where(visible[b], scores[:, b * 128 : (b + 1) * 128], -jnp.inf)
            branch = jnp.exp2(branch - jnp.max(branch, axis=1, keepdims=True))
            factor = weight[b] / jnp.sum(branch, axis=1, keepdims=True)
            shares.append((branch * factor).astype(jnp.bfloat16))
        return jnp.concatenate(shares, axis=1)

    def attend(h, *chips):
        blocks = []
        for c in chips:
            first = (source_of(me, c, 0) // 2) * 2
            blocks += [first, first + 1]
        for d in blocks:

            @pl.when(d != me)
            def _():
                await_bytes(q_got.at[h, d], q_sems.at[h, d])

        halves = [blocks[:4], blocks[4:]]
        scores = [self_scores(half, h) for half in halves]
        weights = [softmax_weights(x) for x in scores]
        self_out = [self_values(x, h) for x in weights]
        scores = [cross_scores(x, h) for x in self_out]
        shares = [cross_weights(x) for x in scores]
        for i, half in enumerate(halves):
            guided = self_out[i] + jnp.dot(
                shares[i], cross_values[h], preferred_element_type=jnp.float32
            )
            guided = guided.astype(jnp.bfloat16)
            for j, d in enumerate(half):
                out_blocks[h, d] = guided[j * tok : (j + 1) * tok]
        lanes = pl.ds(h * HEAD_DIM, HEAD_DIM)
        for d in blocks:

            @pl.when(d != me)
            def _():
                pltpu.make_async_remote_copy(
                    src_ref=out_blocks.at[h, d], dst_ref=out_ref.at[me, :, lanes],
                    send_sem=send_sems.at[6 + h], recv_sem=out_sem,
                    device_id={"seq": d}, device_id_type=MESH,
                ).start()

            @pl.when(d == me)
            def _():
                pltpu.make_async_copy(
                    out_blocks.at[h, me], out_ref.at[me, :, lanes], out_sem
                ).start()

    for h in range(2):
        if h == 1:
            take(1)
        over_chips(parts // 2, functools.partial(attend, h), at_once=4)

    swap.wait_send()
    fetch.wait_send()
    some = pl.ds(0, parts - 1)
    for h in range(2):
        await_bytes(k_got.at[h, some], send_sems.at[h])
        await_bytes(v_got.at[h, some], send_sems.at[2 + h])
        await_bytes(q_got.at[h, some], send_sems.at[4 + h])
        await_bytes(out_blocks.at[h, some], send_sems.at[6 + h])
    await_bytes(scale_got.at[some, 0:2], send_sems.at[8])
    await_bytes(out_ref, out_sem)


def arrange(steps_ref, got_ref, out_ref, sems):
    parts, _, cols = got_ref.shape
    choice = choice_of(steps_ref)
    copies = []
    for d in range(parts):
        worker = d + choice * (across(d) - d)
        lanes = slice(d * cols, (d + 1) * cols)
        copies.append(pltpu.make_async_copy(got_ref.at[worker], out_ref.at[:, lanes], sems.at[d]))
    for copy in copies:
        copy.start()
    for copy in copies:
        copy.wait()


def body(q, k, v, timesteps, norm_gain, cross_gain, prompts, lengths):
    parts = lax.axis_size("seq")
    _, tok, width = q.shape
    cols = width // parts
    text = prompts.shape[3]
    bf16, f32 = jnp.bfloat16, jnp.float32
    hbm = pl.BlockSpec(memory_space=pltpu.HBM)
    vmem = pl.BlockSpec(memory_space=pltpu.VMEM)
    smem = pl.BlockSpec(memory_space=pltpu.SMEM)
    dma = pltpu.SemaphoreType.DMA
    blocks = pltpu.VMEM((2, parts, tok, HEAD_DIM), bf16)
    got = pl.pallas_call(
        functools.partial(kernel, (parts, tok, cols)),
        out_shape=pltpu.VMEM((parts, tok, cols), bf16),
        in_specs=[smem] + [hbm] * 7,
        out_specs=vmem,
        scratch_shapes=[
            pltpu.SMEM((2,), jnp.int32),
            pltpu.VMEM((tok, width), bf16),
            pltpu.VMEM((tok, width), bf16),
            pltpu.VMEM((tok, width), bf16),
            pltpu.VMEM((2, width), bf16),
            pltpu.VMEM((1, cols), bf16),
            blocks, blocks, blocks,
            blocks, blocks, blocks,
            pltpu.VMEM((2, parts * tok, HEAD_DIM), bf16),
            pltpu.VMEM((2, parts * tok, 2 * HEAD_DIM), bf16),
            blocks,
            pltpu.VMEM((8, tok), f32),
            pltpu.VMEM((parts, 8, tok), f32),
            pltpu.VMEM((parts, tok, 128), f32),
            pltpu.VMEM((parts, tok, 128), f32),
            pltpu.VMEM((2, 8, cols), f32),
            pltpu.VMEM((2, 4 * text, cols), bf16),
            pltpu.VMEM((2, 2 * text, HEAD_DIM), bf16),
            pltpu.VMEM((2, 2 * text, HEAD_DIM), bf16),
            dma((6,)),
            dma((2, parts)),
            dma((2, parts)),
            dma((2, parts)),
            dma((parts,)),
            dma((11,)),
            dma,
            dma,
            dma,
            dma,
            pltpu.SemaphoreType.REGULAR,
            pltpu.SemaphoreType.REGULAR,
        ],
        compiler_params=pltpu.CompilerParams(
            collective_id=0, has_side_effects=True, vmem_limit_bytes=44 * 2**20
        ),
        name="guided_attention",
    )(
        timesteps,
        *(
            pltpu.with_memory_space_constraint(x, pltpu.HBM)
            for x in (
                lengths,
                q.reshape(tok, width), k.reshape(tok, width), v.reshape(tok, width),
                norm_gain.reshape(2, width), cross_gain, prompts.reshape(4 * text, cols),
            )
        ),
    )
    out = pl.pallas_call(
        arrange,
        out_shape=jax.ShapeDtypeStruct((tok, width), bf16),
        in_specs=[smem, vmem],
        out_specs=hbm,
        scratch_shapes=[dma((parts,))],
        compiler_params=pltpu.CompilerParams(vmem_limit_bytes=8 * 2**20),
        name="arrange",
    )(timesteps, got)
    return out[None]


def solution(mesh):
    placed = (
        P(("expert", "dp"), "seq", None),
        P(("expert", "dp"), "seq", None),
        P(("expert", "dp"), "seq", None),
        P(("expert", "dp")),
        P("expert", None, None),
        P("expert", "seq"),
        P("expert", None, None, None, "seq"),
        P(),
    )
    return jax.shard_map(
        body,
        mesh=mesh,
        in_specs=placed,
        out_specs=P(("expert", "dp"), "seq", None),
        check_vma=False,
    )
```

```python
import functools
import math

import jax
import jax.numpy as jnp
from jax import lax
from jax.experimental import pallas as pl
from jax.experimental.pallas import tpu as pltpu
from jax.sharding import PartitionSpec as P

HEAD_DIM = 128
BOUNDARY = 875
GUIDANCE = 5.0
EPS = 1e-06
SCORE_SCALE = math.log2(math.e) / math.sqrt(HEAD_DIM)
MESH = pl.DeviceIdType.MESH
ROWS_OF_Y = 4
NT = (((1,), (1,)), ((), ()))


CHIPS = (5, 3, 7, 4, 1, 2, 6, 0)
CHIP_CODE = sum(chip * 8**i for i, chip in enumerate(CHIPS))


def over_chips(count, visit, at_once=1):
    def step(_, code):
        visit(*(code // 8**i % 8 for i in range(at_once)))
        return code // 8**at_once

    lax.fori_loop(0, count // at_once, step, jnp.int32(CHIP_CODE))


def shifted(me, y_steps, x_steps, core_steps):
    y, x, core = me // 4, (me // 2) % 2, me % 2
    y, x, core = (y + y_steps) % ROWS_OF_Y, (x + x_steps) % 2, (core + core_steps) % 2
    return (y * 2 + x) * 2 + core


def source_of(me, chip, core_steps):
    return shifted(me, chip // 2, chip % 2, core_steps)


def target_of(me, chip, core_steps):
    return shifted(me, ROWS_OF_Y - chip // 2, chip % 2, core_steps)


def across(d):
    return d + 2 - 4 * ((d // 2) % 2)


def choice_of(steps_ref):
    routed = jnp.where(steps_ref[0] >= BOUNDARY, 0, 1)
    return jnp.where(routed == lax.axis_index("expert"), 0, 1)


def kernel(
    sizes,
    steps_ref, length_ref, q_ref, k_ref, v_ref, gain_ref, cross_gain_ref, prompt_ref,
    out_ref,
    lengths_ref, q_rows, k_rows, v_rows, gain_rows, cross_rows,
    q_sent, k_sent, v_sent,
    q_got, k_got, v_got,
    k_normed, v_wide, out_blocks,
    scale_own, scale_got, k_scale, q_scale,
    gains, tables, cross_keys, cross_values,
    row_sems, q_sems, k_sems, v_sems, scale_sems, send_sems,
    out_sem, gain_sem, table_own_sem, table_sem, late_sem, late_partner_sem,
):
    parts, tok, cols = sizes
    expert = lax.axis_index("expert")
    me = lax.axis_index("seq")

    choice = choice_of(steps_ref)

    def pick(here, there):
        return lax.select_n(choice == 1, here, there)

    partner = {"expert": 1 - expert, "seq": across(me)}

    own_cols = pl.ds(pl.multiple_of(me * cols, cols), cols)
    local = [
        pltpu.make_async_copy(k_ref, k_rows, row_sems.at[0]),
        pltpu.make_async_copy(gain_ref, gain_rows, row_sems.at[1]),
        pltpu.make_async_copy(cross_gain_ref, cross_rows, row_sems.at[2]),
        pltpu.make_async_copy(q_ref, q_rows, row_sems.at[3]),
        pltpu.make_async_copy(v_ref, v_rows, row_sems.at[4]),
        pltpu.make_async_copy(prompt_ref, tables.at[0], table_own_sem),
        pltpu.make_async_copy(length_ref, lengths_ref, row_sems.at[5]),
    ]
    local[0].start()

    barrier = pltpu.get_barrier_semaphore()

    def signal_group(sem):
        def one(i, carry):
            pl.semaphore_signal(sem, 1, device_id={"seq": (me + i) % parts}, device_id_type=MESH)
            return carry

        lax.fori_loop(1, parts, one, 0)

    scale_got[...] = jnp.zeros_like(scale_got)

    @pl.when(me != 0)
    def _():
        signal_group(barrier)
        pl.semaphore_signal(barrier, 1, device_id=partner, device_id_type=MESH)

    for copy in local[1:]:
        copy.start()

    def stage(rows, sent):
        def one(d, carry):
            here = pl.ds(pl.multiple_of(d * cols, cols), cols)
            there = pl.ds(pl.multiple_of(across(d) * cols, cols), cols)
            both = pick(rows[:, here], rows[:, there])
            for h in range(2):
                sent[h, d] = both[:, h * HEAD_DIM : (h + 1) * HEAD_DIM]
            return carry

        lax.fori_loop(0, parts, one, 0)

    def to_group(send):
        def chip(c):
            for core in range(2):
                send(target_of(me, c, core))

        over_chips(parts // 2 - 1, chip)
        send(shifted(me, 0, 0, 1))

    def sender(sent, got, sems, kind, h):
        def send(d):
            pltpu.make_async_remote_copy(
                src_ref=sent.at[h, d], dst_ref=got.at[h, me],
                send_sem=send_sems.at[2 * kind + h], recv_sem=sems.at[h, me],
                device_id={"seq": d}, device_id_type=MESH,
            ).start()

        return send

    def send_scale(d):
        pltpu.make_async_remote_copy(
            src_ref=scale_own.at[0:2], dst_ref=scale_got.at[me, 0:2],
            send_sem=send_sems.at[8], recv_sem=scale_sems.at[me],
            device_id={"seq": d}, device_id_type=MESH,
        ).start()

    def but_first(send):
        def guarded(d):
            @pl.when(d != 0)
            def _():
                send(d)

        return guarded

    def await_bytes(ref, sem):
        pltpu.make_async_copy(ref, ref, sem).wait()

    local[0].wait()
    stage(k_rows, k_sent)

    @pl.when(me == 0)
    def _():
        pl.semaphore_wait(barrier, parts)
        signal_group(late_sem)
        pl.semaphore_signal(late_partner_sem, 1, device_id=partner, device_id_type=MESH)

    @pl.when(me == 2)
    def _():
        pl.semaphore_wait(barrier, parts - 2)

    @pl.when((me != 0) & (me != 2))
    def _():
        pl.semaphore_wait(barrier, parts - 1)

    send_keys = sender(k_sent, k_got, k_sems, 0, 0)
    to_group(but_first(send_keys))

    def inverse_rms(rows):
        def add(c, total):
            part = rows[:, pl.ds(pl.multiple_of(c * 512, 512), 512)].astype(jnp.float32)
            part = part * part
            return total + (
                (part[:, :128] + part[:, 128:256]) + (part[:, 256:384] + part[:, 384:])
            )

        width = rows.shape[1]
        total = lax.fori_loop(0, width // 512, add, jnp.zeros((tok, 128), jnp.float32))
        mean = jnp.sum(jnp.transpose(total), axis=0, keepdims=True) / width
        return lax.rsqrt(mean + EPS)

    scale_own[0:1, :] = inverse_rms(k_rows)
    local[3].wait()
    scale_own[1:2, :] = inverse_rms(q_rows)
    scale_own[2:8, :] = jnp.zeros((6, tok), jnp.float32)
    scale_got[me] = scale_own[...]

    to_group(but_first(send_scale))

    local[1].wait()
    local[2].wait()
    gains[0, 0:2, :] = gain_rows[:, own_cols].astype(jnp.float32)
    gains[0, 2:3, :] = cross_rows[...].astype(jnp.float32)
    gains[0, 3:8, :] = jnp.zeros((5, cols), jnp.float32)
    swap = pltpu.make_async_remote_copy(
        src_ref=gains.at[0], dst_ref=gains.at[1],
        send_sem=send_sems.at[9], recv_sem=gain_sem,
        device_id=partner, device_id_type=MESH,
    )
    fetch = pltpu.make_async_remote_copy(
        src_ref=prompt_ref, dst_ref=tables.at[1],
        send_sem=send_sems.at[10], recv_sem=table_sem,
        device_id=partner, device_id_type=MESH,
    )

    @pl.when(me == 2)
    def _():
        pl.semaphore_wait(late_partner_sem, 1)

    swap.start()
    fetch.start()
    local[4].wait()
    stage(v_rows, v_sent)
    send_values = sender(v_sent, v_got, v_sems, 1, 0)
    to_group(but_first(send_values))
    stage(q_rows, q_sent)

    @pl.when(me != 0)
    def _():
        pl.semaphore_wait(late_sem, 1)
        send_keys(0)
        send_scale(0)
        send_values(0)

    to_group(sender(q_sent, q_got, q_sems, 2, 0))
    to_group(sender(k_sent, k_got, k_sems, 0, 1))
    to_group(sender(v_sent, v_got, v_sems, 1, 1))
    to_group(sender(q_sent, q_got, q_sems, 2, 1))
    for h in range(2):
        k_got[h, me] = k_sent[h, me]
        v_got[h, me] = v_sent[h, me]
        q_got[h, me] = q_sent[h, me]
    v_wide[:, :, HEAD_DIM:] = jnp.ones((2, parts * tok, HEAD_DIM), jnp.bfloat16)

    swap.wait_recv()

    def from_group(take):
        def chip(c):
            for core in range(2):
                take(source_of(me, c, core))

        over_chips(parts // 2, chip)

    def await_scale(s):
        @pl.when(s != me)
        def _():
            await_bytes(scale_got.at[s, 0:2], scale_sems.at[s])

    from_group(await_scale)
    flipped = jnp.transpose(scale_got[...].reshape(parts * 8, tok))
    for s in range(parts):
        k_scale[s] = jnp.broadcast_to(flipped[:, 8 * s : 8 * s + 1], (tok, 128))
        q_scale[s] = jnp.broadcast_to(flipped[:, 8 * s + 1 : 8 * s + 2], (tok, 128))

    chosen = gains[choice]
    q_gain = chosen[0:1, :] * SCORE_SCALE
    k_gain = chosen[1:2, :]
    cross_gain = chosen[2:3, :] * SCORE_SCALE

    def take_keys(s, h):
        @pl.when(s != me)
        def _():
            await_bytes(k_got.at[h, s], k_sems.at[h, s])

        lanes = slice(h * HEAD_DIM, (h + 1) * HEAD_DIM)
        normed = k_got[h, s].astype(jnp.float32) * k_scale[s] * k_gain[:, lanes]
        k_normed[h, pl.ds(pl.multiple_of(s * tok, tok), tok), :] = normed.astype(jnp.bfloat16)

    def take_values(s, h):
        @pl.when(s != me)
        def _():
            await_bytes(v_got.at[h, s], v_sems.at[h, s])

        v_wide[h, pl.ds(pl.multiple_of(s * tok, tok), tok), :HEAD_DIM] = v_got[h, s]

    def take(h):
        from_group(lambda s: take_keys(s, h))
        from_group(lambda s: take_values(s, h))

    take(0)

    local[5].wait()
    local[6].wait()
    fetch.wait_recv()
    for h in range(2):
        lanes = slice(h * HEAD_DIM, (h + 1) * HEAD_DIM)
        for b in range(2):
            rows = slice(b * 128, (b + 1) * 128)
            cross_keys[h, rows, :] = tables[choice, b * 256 : b * 256 + 128, lanes]
            cross_values[h, rows, :] = tables[choice, b * 256 + 128 : b * 256 + 256, lanes]

    position = lax.broadcasted_iota(jnp.int32, (4 * tok, 128), 1)
    visible = [position < lengths_ref[b] for b in range(2)]
    weight = (GUIDANCE, 1.0 - GUIDANCE)

    def self_scores(blocks, h):
        lanes = slice(h * HEAD_DIM, (h + 1) * HEAD_DIM)
        query = jnp.concatenate(
            [
                (q_got[h, d].astype(jnp.float32) * q_scale[d] * q_gain[:, lanes]).astype(
                    jnp.bfloat16
                )
                for d in blocks
            ],
            axis=0,
        )
        return lax.dot_general(query, k_normed[h], NT, preferred_element_type=jnp.float32)

    def softmax_weights(scores):
        peak = jnp.max(scores, axis=1, keepdims=True)
        return jnp.exp2(scores - peak).astype(jnp.bfloat16)

    def self_values(weights, h):
        sums = jnp.dot(weights, v_wide[h], preferred_element_type=jnp.float32)
        self_out = (sums[:, :HEAD_DIM] / sums[:, HEAD_DIM:]).astype(jnp.bfloat16)
        return self_out.astype(jnp.float32)

    def cross_scores(self_out, h):
        lanes = slice(h * HEAD_DIM, (h + 1) * HEAD_DIM)
        mean = jnp.mean(self_out * self_out, axis=1, keepdims=True)
        query = self_out * lax.rsqrt(mean + EPS) * cross_gain[:, lanes]
        return lax.dot_general(
            query.astype(jnp.bfloat16), cross_keys[h], NT, preferred_element_type=jnp.float32
        )

    def cross_weights(scores):
        shares = []
        for b in range(2):
            branch = jnp.where(visible[b], scores[:, b * 128 : (b + 1) * 128], -jnp.inf)
            branch = jnp.exp2(branch - jnp.max(branch, axis=1, keepdims=True))
            factor = weight[b] / jnp.sum(branch, axis=1, keepdims=True)
            shares.append((branch * factor).astype(jnp.bfloat16))
        return jnp.concatenate(shares, axis=1)

    late_chip = ((ROWS_OF_Y - me // 4) % ROWS_OF_Y) * 2 + (me // 2) % 2
    early = functools.reduce(
        jnp.logical_or, [late_chip == c for c in CHIPS[: len(CHIPS) // 2]]
    )
    stand_in = (source_of(me, CHIPS[len(CHIPS) // 2], 0) // 2) * 2

    def put_off(d):
        swapped = jnp.where(d == 0, stand_in, jnp.where(d == stand_in, 0, d))
        return jnp.where(early, swapped, d)

    def attend(h, *chips):
        blocks = []
        for c in chips:
            first = (source_of(me, c, 0) // 2) * 2
            blocks += [first, first + 1]
        if h == 1:
            blocks = [put_off(d) for d in blocks]
        for d in blocks:

            @pl.when(d != me)
            def _():
                await_bytes(q_got.at[h, d], q_sems.at[h, d])

        halves = [blocks[:4], blocks[4:]]
        scores = [self_scores(half, h) for half in halves]
        weights = [softmax_weights(x) for x in scores]
        self_out = [self_values(x, h) for x in weights]
        scores = [cross_scores(x, h) for x in self_out]
        shares = [cross_weights(x) for x in scores]
        for i, half in enumerate(halves):
            guided = self_out[i] + jnp.dot(
                shares[i], cross_values[h], preferred_element_type=jnp.float32
            )
            guided = guided.astype(jnp.bfloat16)
            for j, d in enumerate(half):
                out_blocks[h, d] = guided[j * tok : (j + 1) * tok]
        lanes = pl.ds(h * HEAD_DIM, HEAD_DIM)
        for d in blocks:

            @pl.when(d != me)
            def _():
                pltpu.make_async_remote_copy(
                    src_ref=out_blocks.at[h, d], dst_ref=out_ref.at[me, :, lanes],
                    send_sem=send_sems.at[6 + h], recv_sem=out_sem,
                    device_id={"seq": d}, device_id_type=MESH,
                ).start()

            @pl.when(d == me)
            def _():
                pltpu.make_async_copy(
                    out_blocks.at[h, me], out_ref.at[me, :, lanes], out_sem
                ).start()

    for h in range(2):
        if h == 1:
            take(1)
        over_chips(parts // 2, functools.partial(attend, h), at_once=4)

    swap.wait_send()
    fetch.wait_send()
    some = pl.ds(0, parts - 1)
    for h in range(2):
        await_bytes(k_got.at[h, some], send_sems.at[h])
        await_bytes(v_got.at[h, some], send_sems.at[2 + h])
        await_bytes(q_got.at[h, some], send_sems.at[4 + h])
        await_bytes(out_blocks.at[h, some], send_sems.at[6 + h])
    await_bytes(scale_got.at[some, 0:2], send_sems.at[8])
    await_bytes(out_ref, out_sem)


def arrange(steps_ref, got_ref, out_ref, sems):
    parts, _, cols = got_ref.shape
    choice = choice_of(steps_ref)
    copies = []
    for d in range(parts):
        worker = d + choice * (across(d) - d)
        lanes = slice(d * cols, (d + 1) * cols)
        copies.append(pltpu.make_async_copy(got_ref.at[worker], out_ref.at[:, lanes], sems.at[d]))
    for copy in copies:
        copy.start()
    for copy in copies:
        copy.wait()


def body(q, k, v, timesteps, norm_gain, cross_gain, prompts, lengths):
    parts = lax.axis_size("seq")
    _, tok, width = q.shape
    cols = width // parts
    text = prompts.shape[3]
    bf16, f32 = jnp.bfloat16, jnp.float32
    hbm = pl.BlockSpec(memory_space=pltpu.HBM)
    vmem = pl.BlockSpec(memory_space=pltpu.VMEM)
    smem = pl.BlockSpec(memory_space=pltpu.SMEM)
    dma = pltpu.SemaphoreType.DMA
    blocks = pltpu.VMEM((2, parts, tok, HEAD_DIM), bf16)
    got = pl.pallas_call(
        functools.partial(kernel, (parts, tok, cols)),
        out_shape=pltpu.VMEM((parts, tok, cols), bf16),
        in_specs=[smem] + [hbm] * 7,
        out_specs=vmem,
        scratch_shapes=[
            pltpu.SMEM((2,), jnp.int32),
            pltpu.VMEM((tok, width), bf16),
            pltpu.VMEM((tok, width), bf16),
            pltpu.VMEM((tok, width), bf16),
            pltpu.VMEM((2, width), bf16),
            pltpu.VMEM((1, cols), bf16),
            blocks, blocks, blocks,
            blocks, blocks, blocks,
            pltpu.VMEM((2, parts * tok, HEAD_DIM), bf16),
            pltpu.VMEM((2, parts * tok, 2 * HEAD_DIM), bf16),
            blocks,
            pltpu.VMEM((8, tok), f32),
            pltpu.VMEM((parts, 8, tok), f32),
            pltpu.VMEM((parts, tok, 128), f32),
            pltpu.VMEM((parts, tok, 128), f32),
            pltpu.VMEM((2, 8, cols), f32),
            pltpu.VMEM((2, 4 * text, cols), bf16),
            pltpu.VMEM((2, 2 * text, HEAD_DIM), bf16),
            pltpu.VMEM((2, 2 * text, HEAD_DIM), bf16),
            dma((6,)),
            dma((2, parts)),
            dma((2, parts)),
            dma((2, parts)),
            dma((parts,)),
            dma((11,)),
            dma,
            dma,
            dma,
            dma,
            pltpu.SemaphoreType.REGULAR,
            pltpu.SemaphoreType.REGULAR,
        ],
        compiler_params=pltpu.CompilerParams(
            collective_id=0, has_side_effects=True, vmem_limit_bytes=44 * 2**20
        ),
        name="guided_attention",
    )(
        timesteps,
        *(
            pltpu.with_memory_space_constraint(x, pltpu.HBM)
            for x in (
                lengths,
                q.reshape(tok, width), k.reshape(tok, width), v.reshape(tok, width),
                norm_gain.reshape(2, width), cross_gain, prompts.reshape(4 * text, cols),
            )
        ),
    )
    out = pl.pallas_call(
        arrange,
        out_shape=jax.ShapeDtypeStruct((tok, width), bf16),
        in_specs=[smem, vmem],
        out_specs=hbm,
        scratch_shapes=[dma((parts,))],
        compiler_params=pltpu.CompilerParams(vmem_limit_bytes=8 * 2**20),
        name="arrange",
    )(timesteps, got)
    return out[None]


def solution(mesh):
    placed = (
        P(("expert", "dp"), "seq", None),
        P(("expert", "dp"), "seq", None),
        P(("expert", "dp"), "seq", None),
        P(("expert", "dp")),
        P("expert", None, None),
        P("expert", "seq"),
        P("expert", None, None, None, "seq"),
        P(),
    )
    return jax.shard_map(
        body,
        mesh=mesh,
        in_specs=placed,
        out_specs=P(("expert", "dp"), "seq", None),
        check_vma=False,
    )
```

```python
import functools
import math

import jax
import jax.numpy as jnp
from jax import lax
from jax.experimental import pallas as pl
from jax.experimental.pallas import tpu as pltpu
from jax.sharding import PartitionSpec as P

HEAD_DIM = 128
BOUNDARY = 875
GUIDANCE = 5.0
EPS = 1e-06
SCORE_SCALE = math.log2(math.e) / math.sqrt(HEAD_DIM)
MESH = pl.DeviceIdType.MESH
ROWS_OF_Y = 4
NT = (((1,), (1,)), ((), ()))


CHIPS = (5, 3, 7, 4, 1, 2, 6, 0)
CHIP_CODE = sum(chip * 8**i for i, chip in enumerate(CHIPS))


def over_chips(count, visit, at_once=1):
    def step(_, code):
        visit(*(code // 8**i % 8 for i in range(at_once)))
        return code // 8**at_once

    lax.fori_loop(0, count // at_once, step, jnp.int32(CHIP_CODE))


def shifted(me, y_steps, x_steps, core_steps):
    y, x, core = me // 4, (me // 2) % 2, me % 2
    y, x, core = (y + y_steps) % ROWS_OF_Y, (x + x_steps) % 2, (core + core_steps) % 2
    return (y * 2 + x) * 2 + core


def source_of(me, chip, core_steps):
    return shifted(me, chip // 2, chip % 2, core_steps)


def target_of(me, chip, core_steps):
    return shifted(me, ROWS_OF_Y - chip // 2, chip % 2, core_steps)


def across(d):
    return d + 2 - 4 * ((d // 2) % 2)


def choice_of(steps_ref):
    routed = jnp.where(steps_ref[0] >= BOUNDARY, 0, 1)
    return jnp.where(routed == lax.axis_index("expert"), 0, 1)


def kernel(
    sizes,
    steps_ref, length_ref, q_ref, k_ref, v_ref, gain_ref, cross_gain_ref, prompt_ref,
    out_ref,
    lengths_ref, q_rows, k_rows, v_rows, gain_rows, cross_rows,
    q_sent, k_sent, v_sent,
    q_got, k_got, v_got,
    k_normed, v_wide, out_blocks,
    scale_own, scale_got, k_scale, q_scale,
    gains, tables, cross_keys, cross_values,
    row_sems, q_sems, k_sems, v_sems, scale_sems, send_sems,
    out_sem, gain_sem, table_own_sem, table_sem, late_sem, late_partner_sem,
):
    parts, tok, cols = sizes
    expert = lax.axis_index("expert")
    me = lax.axis_index("seq")

    choice = choice_of(steps_ref)

    def pick(here, there):
        return lax.select_n(choice == 1, here, there)

    partner = {"expert": 1 - expert, "seq": across(me)}

    own_cols = pl.ds(pl.multiple_of(me * cols, cols), cols)
    local = [
        pltpu.make_async_copy(k_ref, k_rows, row_sems.at[0]),
        pltpu.make_async_copy(gain_ref, gain_rows, row_sems.at[1]),
        pltpu.make_async_copy(cross_gain_ref, cross_rows, row_sems.at[2]),
        pltpu.make_async_copy(q_ref, q_rows, row_sems.at[3]),
        pltpu.make_async_copy(v_ref, v_rows, row_sems.at[4]),
        pltpu.make_async_copy(prompt_ref, tables.at[0], table_own_sem),
        pltpu.make_async_copy(length_ref, lengths_ref, row_sems.at[5]),
    ]
    local[0].start()

    barrier = pltpu.get_barrier_semaphore()

    def signal_group(sem):
        def one(i, carry):
            pl.semaphore_signal(sem, 1, device_id={"seq": (me + i) % parts}, device_id_type=MESH)
            return carry

        lax.fori_loop(1, parts, one, 0)

    scale_got[...] = jnp.zeros_like(scale_got)

    @pl.when(me != 0)
    def _():
        signal_group(barrier)
        pl.semaphore_signal(barrier, 1, device_id=partner, device_id_type=MESH)

    for copy in local[1:]:
        copy.start()

    def stage(rows, sent):
        def one(d, carry):
            here = pl.ds(pl.multiple_of(d * cols, cols), cols)
            there = pl.ds(pl.multiple_of(across(d) * cols, cols), cols)
            both = pick(rows[:, here], rows[:, there])
            for h in range(2):
                sent[h, d] = both[:, h * HEAD_DIM : (h + 1) * HEAD_DIM]
            return carry

        lax.fori_loop(0, parts, one, 0)

    def to_group(send):
        def chip(c):
            for core in range(2):
                send(target_of(me, c, core))

        over_chips(parts // 2 - 1, chip)
        send(shifted(me, 0, 0, 1))

    def sender(sent, got, sems, kind, h):
        def send(d):
            pltpu.make_async_remote_copy(
                src_ref=sent.at[h, d], dst_ref=got.at[h, me],
                send_sem=send_sems.at[2 * kind + h], recv_sem=sems.at[h, me],
                device_id={"seq": d}, device_id_type=MESH,
            ).start()

        return send

    def send_scale(d):
        pltpu.make_async_remote_copy(
            src_ref=scale_own.at[0:2], dst_ref=scale_got.at[me, 0:2],
            send_sem=send_sems.at[8], recv_sem=scale_sems.at[me],
            device_id={"seq": d}, device_id_type=MESH,
        ).start()

    def but_first(send):
        def guarded(d):
            @pl.when(d != 0)
            def _():
                send(d)

        return guarded

    def await_bytes(ref, sem):
        pltpu.make_async_copy(ref, ref, sem).wait()

    local[0].wait()
    stage(k_rows, k_sent)

    @pl.when(me == 0)
    def _():
        pl.semaphore_wait(barrier, parts)
        signal_group(late_sem)
        pl.semaphore_signal(late_partner_sem, 1, device_id=partner, device_id_type=MESH)

    @pl.when(me == 2)
    def _():
        pl.semaphore_wait(barrier, parts - 2)

    @pl.when((me != 0) & (me != 2))
    def _():
        pl.semaphore_wait(barrier, parts - 1)

    send_keys = sender(k_sent, k_got, k_sems, 0, 0)
    to_group(but_first(send_keys))

    def inverse_rms(rows):
        def add(c, total):
            part = rows[:, pl.ds(pl.multiple_of(c * 512, 512), 512)].astype(jnp.float32)
            part = part * part
            return total + (
                (part[:, :128] + part[:, 128:256]) + (part[:, 256:384] + part[:, 384:])
            )

        width = rows.shape[1]
        total = lax.fori_loop(0, width // 512, add, jnp.zeros((tok, 128), jnp.float32))
        mean = jnp.sum(jnp.transpose(total), axis=0, keepdims=True) / width
        return lax.rsqrt(mean + EPS)

    scale_own[0:1, :] = inverse_rms(k_rows)
    local[3].wait()
    scale_own[1:2, :] = inverse_rms(q_rows)
    scale_own[2:8, :] = jnp.zeros((6, tok), jnp.float32)
    scale_got[me] = scale_own[...]

    to_group(but_first(send_scale))

    local[1].wait()
    local[2].wait()
    gains[0, 0:2, :] = gain_rows[:, own_cols].astype(jnp.float32)
    gains[0, 2:3, :] = cross_rows[...].astype(jnp.float32)
    gains[0, 3:8, :] = jnp.zeros((5, cols), jnp.float32)
    swap = pltpu.make_async_remote_copy(
        src_ref=gains.at[0], dst_ref=gains.at[1],
        send_sem=send_sems.at[9], recv_sem=gain_sem,
        device_id=partner, device_id_type=MESH,
    )
    fetch = pltpu.make_async_remote_copy(
        src_ref=prompt_ref, dst_ref=tables.at[1],
        send_sem=send_sems.at[10], recv_sem=table_sem,
        device_id=partner, device_id_type=MESH,
    )

    @pl.when(me == 2)
    def _():
        pl.semaphore_wait(late_partner_sem, 1)

    swap.start()
    fetch.start()
    local[4].wait()
    stage(v_rows, v_sent)
    send_values = sender(v_sent, v_got, v_sems, 1, 0)
    to_group(but_first(send_values))
    stage(q_rows, q_sent)

    @pl.when(me != 0)
    def _():
        pl.semaphore_wait(late_sem, 1)
        send_keys(0)
        send_scale(0)
        send_values(0)

    to_group(sender(q_sent, q_got, q_sems, 2, 0))
    to_group(sender(k_sent, k_got, k_sems, 0, 1))
    to_group(sender(v_sent, v_got, v_sems, 1, 1))
    to_group(sender(q_sent, q_got, q_sems, 2, 1))
    for h in range(2):
        k_got[h, me] = k_sent[h, me]
        v_got[h, me] = v_sent[h, me]
        q_got[h, me] = q_sent[h, me]
    v_wide[:, :, HEAD_DIM:] = jnp.ones((2, parts * tok, HEAD_DIM), jnp.bfloat16)

    swap.wait_recv()

    def from_group(take):
        def chip(c):
            for core in range(2):
                take(source_of(me, c, core))

        over_chips(parts // 2, chip)

    def await_scale(s):
        @pl.when(s != me)
        def _():
            await_bytes(scale_got.at[s, 0:2], scale_sems.at[s])

    from_group(await_scale)
    flipped = jnp.transpose(scale_got[...].reshape(parts * 8, tok))
    for s in range(parts):
        k_scale[s] = jnp.broadcast_to(flipped[:, 8 * s : 8 * s + 1], (tok, 128))
        q_scale[s] = jnp.broadcast_to(flipped[:, 8 * s + 1 : 8 * s + 2], (tok, 128))

    chosen = gains[choice]
    q_gain = chosen[0:1, :] * SCORE_SCALE
    k_gain = chosen[1:2, :]
    cross_gain = chosen[2:3, :] * SCORE_SCALE

    def take_keys(s, h):
        @pl.when(s != me)
        def _():
            await_bytes(k_got.at[h, s], k_sems.at[h, s])

        lanes = slice(h * HEAD_DIM, (h + 1) * HEAD_DIM)
        normed = k_got[h, s].astype(jnp.float32) * k_scale[s] * k_gain[:, lanes]
        k_normed[h, pl.ds(pl.multiple_of(s * tok, tok), tok), :] = normed.astype(jnp.bfloat16)

    def take_values(s, h):
        @pl.when(s != me)
        def _():
            await_bytes(v_got.at[h, s], v_sems.at[h, s])

        v_wide[h, pl.ds(pl.multiple_of(s * tok, tok), tok), :HEAD_DIM] = v_got[h, s]

    def take(h):
        from_group(lambda s: take_keys(s, h))
        from_group(lambda s: take_values(s, h))

    take(0)

    local[5].wait()
    local[6].wait()
    fetch.wait_recv()
    for h in range(2):
        lanes = slice(h * HEAD_DIM, (h + 1) * HEAD_DIM)
        for b in range(2):
            rows = slice(b * 128, (b + 1) * 128)
            cross_keys[h, rows, :] = tables[choice, b * 256 : b * 256 + 128, lanes]
            cross_values[h, rows, :] = tables[choice, b * 256 + 128 : b * 256 + 256, lanes]

    position = lax.broadcasted_iota(jnp.int32, (4 * tok, 128), 1)
    visible = [position < lengths_ref[b] for b in range(2)]
    weight = (GUIDANCE, 1.0 - GUIDANCE)

    def self_scores(blocks, h):
        lanes = slice(h * HEAD_DIM, (h + 1) * HEAD_DIM)
        query = jnp.concatenate(
            [
                (q_got[h, d].astype(jnp.float32) * q_scale[d] * q_gain[:, lanes]).astype(
                    jnp.bfloat16
                )
                for d in blocks
            ],
            axis=0,
        )
        return lax.dot_general(query, k_normed[h], NT, preferred_element_type=jnp.float32)

    def softmax_weights(scores):
        peak = jnp.max(scores, axis=1, keepdims=True)
        return jnp.exp2(scores - peak).astype(jnp.bfloat16)

    def self_values(weights, h):
        sums = jnp.dot(weights, v_wide[h], preferred_element_type=jnp.float32)
        self_out = (sums[:, :HEAD_DIM] / sums[:, HEAD_DIM:]).astype(jnp.bfloat16)
        return self_out.astype(jnp.float32)

    def cross_scores(self_out, h):
        lanes = slice(h * HEAD_DIM, (h + 1) * HEAD_DIM)
        mean = jnp.mean(self_out * self_out, axis=1, keepdims=True)
        query = self_out * lax.rsqrt(mean + EPS) * cross_gain[:, lanes]
        return lax.dot_general(
            query.astype(jnp.bfloat16), cross_keys[h], NT, preferred_element_type=jnp.float32
        )

    def cross_weights(scores):
        shares = []
        for b in range(2):
            branch = jnp.where(visible[b], scores[:, b * 128 : (b + 1) * 128], -jnp.inf)
            branch = jnp.exp2(branch - jnp.max(branch, axis=1, keepdims=True))
            factor = weight[b] / jnp.sum(branch, axis=1, keepdims=True)
            shares.append((branch * factor).astype(jnp.bfloat16))
        return jnp.concatenate(shares, axis=1)

    late_chip = ((ROWS_OF_Y - me // 4) % ROWS_OF_Y) * 2 + (me // 2) % 2
    half = len(CHIPS) // 2
    far = late_chip == CHIPS[half - 1]
    near = functools.reduce(jnp.logical_or, [late_chip == c for c in CHIPS[half:-1]])
    give = jnp.where(far, 0, 1)
    take_up = jnp.where(
        far,
        (source_of(me, CHIPS[half], 0) // 2) * 2,
        (source_of(me, CHIPS[half - 1], 0) // 2) * 2 + 1,
    )

    def put_off(d):
        swapped = jnp.where(d == give, take_up, jnp.where(d == take_up, give, d))
        return jnp.where(far | near, swapped, d)

    def attend(h, *chips):
        blocks = []
        for c in chips:
            first = (source_of(me, c, 0) // 2) * 2
            blocks += [first, first + 1]
        if h == 1:
            blocks = [put_off(d) for d in blocks]
        for d in blocks:

            @pl.when(d != me)
            def _():
                await_bytes(q_got.at[h, d], q_sems.at[h, d])

        halves = [blocks[:4], blocks[4:]]
        scores = [self_scores(half, h) for half in halves]
        weights = [softmax_weights(x) for x in scores]
        self_out = [self_values(x, h) for x in weights]
        scores = [cross_scores(x, h) for x in self_out]
        shares = [cross_weights(x) for x in scores]
        for i, half in enumerate(halves):
            guided = self_out[i] + jnp.dot(
                shares[i], cross_values[h], preferred_element_type=jnp.float32
            )
            guided = guided.astype(jnp.bfloat16)
            for j, d in enumerate(half):
                out_blocks[h, d] = guided[j * tok : (j + 1) * tok]
        lanes = pl.ds(h * HEAD_DIM, HEAD_DIM)

        def send_out(d):
            pltpu.make_async_remote_copy(
                src_ref=out_blocks.at[h, d], dst_ref=out_ref.at[me, :, lanes],
                send_sem=send_sems.at[6 + h], recv_sem=out_sem,
                device_id={"seq": d}, device_id_type=MESH,
            ).start()

        holds_first = functools.reduce(jnp.logical_or, [d == 0 for d in blocks])

        @pl.when(holds_first & (me != 0))
        def _():
            send_out(0)

        for d in blocks:

            @pl.when((d != me) & (d != 0))
            def _():
                send_out(d)

            @pl.when(d == me)
            def _():
                pltpu.make_async_copy(
                    out_blocks.at[h, me], out_ref.at[me, :, lanes], out_sem
                ).start()

    for h in range(2):
        if h == 1:
            take(1)
        over_chips(parts // 2, functools.partial(attend, h), at_once=4)

    swap.wait_send()
    fetch.wait_send()
    some = pl.ds(0, parts - 1)
    for h in range(2):
        await_bytes(k_got.at[h, some], send_sems.at[h])
        await_bytes(v_got.at[h, some], send_sems.at[2 + h])
        await_bytes(q_got.at[h, some], send_sems.at[4 + h])
        await_bytes(out_blocks.at[h, some], send_sems.at[6 + h])
    await_bytes(scale_got.at[some, 0:2], send_sems.at[8])
    await_bytes(out_ref, out_sem)


def arrange(steps_ref, got_ref, out_ref, sems):
    parts, _, cols = got_ref.shape
    choice = choice_of(steps_ref)
    copies = []
    for d in range(parts):
        worker = d + choice * (across(d) - d)
        lanes = slice(d * cols, (d + 1) * cols)
        copies.append(pltpu.make_async_copy(got_ref.at[worker], out_ref.at[:, lanes], sems.at[d]))
    for copy in copies:
        copy.start()
    for copy in copies:
        copy.wait()


def body(q, k, v, timesteps, norm_gain, cross_gain, prompts, lengths):
    parts = lax.axis_size("seq")
    _, tok, width = q.shape
    cols = width // parts
    text = prompts.shape[3]
    bf16, f32 = jnp.bfloat16, jnp.float32
    hbm = pl.BlockSpec(memory_space=pltpu.HBM)
    vmem = pl.BlockSpec(memory_space=pltpu.VMEM)
    smem = pl.BlockSpec(memory_space=pltpu.SMEM)
    dma = pltpu.SemaphoreType.DMA
    blocks = pltpu.VMEM((2, parts, tok, HEAD_DIM), bf16)
    got = pl.pallas_call(
        functools.partial(kernel, (parts, tok, cols)),
        out_shape=pltpu.VMEM((parts, tok, cols), bf16),
        in_specs=[smem] + [hbm] * 7,
        out_specs=vmem,
        scratch_shapes=[
            pltpu.SMEM((2,), jnp.int32),
            pltpu.VMEM((tok, width), bf16),
            pltpu.VMEM((tok, width), bf16),
            pltpu.VMEM((tok, width), bf16),
            pltpu.VMEM((2, width), bf16),
            pltpu.VMEM((1, cols), bf16),
            blocks, blocks, blocks,
            blocks, blocks, blocks,
            pltpu.VMEM((2, parts * tok, HEAD_DIM), bf16),
            pltpu.VMEM((2, parts * tok, 2 * HEAD_DIM), bf16),
            blocks,
            pltpu.VMEM((8, tok), f32),
            pltpu.VMEM((parts, 8, tok), f32),
            pltpu.VMEM((parts, tok, 128), f32),
            pltpu.VMEM((parts, tok, 128), f32),
            pltpu.VMEM((2, 8, cols), f32),
            pltpu.VMEM((2, 4 * text, cols), bf16),
            pltpu.VMEM((2, 2 * text, HEAD_DIM), bf16),
            pltpu.VMEM((2, 2 * text, HEAD_DIM), bf16),
            dma((6,)),
            dma((2, parts)),
            dma((2, parts)),
            dma((2, parts)),
            dma((parts,)),
            dma((11,)),
            dma,
            dma,
            dma,
            dma,
            pltpu.SemaphoreType.REGULAR,
            pltpu.SemaphoreType.REGULAR,
        ],
        compiler_params=pltpu.CompilerParams(
            collective_id=0, has_side_effects=True, vmem_limit_bytes=44 * 2**20
        ),
        name="guided_attention",
    )(
        timesteps,
        *(
            pltpu.with_memory_space_constraint(x, pltpu.HBM)
            for x in (
                lengths,
                q.reshape(tok, width), k.reshape(tok, width), v.reshape(tok, width),
                norm_gain.reshape(2, width), cross_gain, prompts.reshape(4 * text, cols),
            )
        ),
    )
    out = pl.pallas_call(
        arrange,
        out_shape=jax.ShapeDtypeStruct((tok, width), bf16),
        in_specs=[smem, vmem],
        out_specs=hbm,
        scratch_shapes=[dma((parts,))],
        compiler_params=pltpu.CompilerParams(vmem_limit_bytes=8 * 2**20),
        name="arrange",
    )(timesteps, got)
    return out[None]


def solution(mesh):
    placed = (
        P(("expert", "dp"), "seq", None),
        P(("expert", "dp"), "seq", None),
        P(("expert", "dp"), "seq", None),
        P(("expert", "dp")),
        P("expert", None, None),
        P("expert", "seq"),
        P("expert", None, None, None, "seq"),
        P(),
    )
    return jax.shard_map(
        body,
        mesh=mesh,
        in_specs=placed,
        out_specs=P(("expert", "dp"), "seq", None),
        check_vma=False,
    )
```

```python
import functools
import math

import jax
import jax.numpy as jnp
from jax import lax
from jax.experimental import pallas as pl
from jax.experimental.pallas import tpu as pltpu
from jax.sharding import PartitionSpec as P

HEAD_DIM = 128
BOUNDARY = 875
GUIDANCE = 5.0
EPS = 1e-06
SCORE_SCALE = math.log2(math.e) / math.sqrt(HEAD_DIM)
MESH = pl.DeviceIdType.MESH
ROWS_OF_Y = 4
NT = (((1,), (1,)), ((), ()))


CHIPS = (5, 3, 7, 4, 1, 2, 6, 0)
CHIP_CODE = sum(chip * 8**i for i, chip in enumerate(CHIPS))


def over_chips(count, visit, at_once=1):
    def step(_, code):
        visit(*(code // 8**i % 8 for i in range(at_once)))
        return code // 8**at_once

    lax.fori_loop(0, count // at_once, step, jnp.int32(CHIP_CODE))


def shifted(me, y_steps, x_steps, core_steps):
    y, x, core = me // 4, (me // 2) % 2, me % 2
    y, x, core = (y + y_steps) % ROWS_OF_Y, (x + x_steps) % 2, (core + core_steps) % 2
    return (y * 2 + x) * 2 + core


def source_of(me, chip, core_steps):
    return shifted(me, chip // 2, chip % 2, core_steps)


def target_of(me, chip, core_steps):
    return shifted(me, ROWS_OF_Y - chip // 2, chip % 2, core_steps)


def across(d):
    return d + 2 - 4 * ((d // 2) % 2)


def choice_of(steps_ref):
    routed = jnp.where(steps_ref[0] >= BOUNDARY, 0, 1)
    return jnp.where(routed == lax.axis_index("expert"), 0, 1)


def kernel(
    sizes,
    steps_ref, length_ref, q_ref, k_ref, v_ref, gain_ref, cross_gain_ref, prompt_ref,
    out_ref,
    lengths_ref, q_rows, k_rows, v_rows, gain_rows, cross_rows,
    q_sent, k_sent, v_sent,
    q_got, k_got, v_got,
    k_normed, v_wide, out_blocks,
    scale_own, scale_got, k_scale, q_scale,
    gains, tables, cross_keys, cross_values,
    row_sems, q_sems, k_sems, v_sems, scale_sems, send_sems,
    out_sem, gain_sem, table_own_sem, table_sem, late_sem, late_partner_sem,
):
    parts, tok, cols = sizes
    expert = lax.axis_index("expert")
    me = lax.axis_index("seq")

    choice = choice_of(steps_ref)

    def pick(here, there):
        return lax.select_n(choice == 1, here, there)

    partner = {"expert": 1 - expert, "seq": across(me)}

    own_cols = pl.ds(pl.multiple_of(me * cols, cols), cols)
    local = [
        pltpu.make_async_copy(k_ref, k_rows, row_sems.at[0]),
        pltpu.make_async_copy(gain_ref, gain_rows, row_sems.at[1]),
        pltpu.make_async_copy(cross_gain_ref, cross_rows, row_sems.at[2]),
        pltpu.make_async_copy(q_ref, q_rows, row_sems.at[3]),
        pltpu.make_async_copy(v_ref, v_rows, row_sems.at[4]),
        pltpu.make_async_copy(prompt_ref, tables.at[0], table_own_sem),
        pltpu.make_async_copy(length_ref, lengths_ref, row_sems.at[5]),
    ]
    local[0].start()

    barrier = pltpu.get_barrier_semaphore()

    def signal_group(sem):
        def one(i, carry):
            pl.semaphore_signal(sem, 1, device_id={"seq": (me + i) % parts}, device_id_type=MESH)
            return carry

        lax.fori_loop(1, parts, one, 0)

    scale_got[...] = jnp.zeros_like(scale_got)

    @pl.when(me != 0)
    def _():
        signal_group(barrier)
        pl.semaphore_signal(barrier, 1, device_id=partner, device_id_type=MESH)

    for copy in local[1:]:
        copy.start()

    def stage(rows, sent, heads):
        def one(d, carry):
            for h in heads:
                here = pl.multiple_of(d * cols + h * HEAD_DIM, HEAD_DIM)
                there = pl.multiple_of(across(d) * cols + h * HEAD_DIM, HEAD_DIM)
                sent[h, d] = pick(rows[:, pl.ds(here, HEAD_DIM)], rows[:, pl.ds(there, HEAD_DIM)])
            return carry

        lax.fori_loop(0, parts, one, 0)

    def to_group(send):
        def chip(c):
            for core in range(2):
                send(target_of(me, c, core))

        over_chips(parts // 2 - 1, chip)
        send(shifted(me, 0, 0, 1))

    def sender(sent, got, sems, kind, h):
        def send(d):
            pltpu.make_async_remote_copy(
                src_ref=sent.at[h, d], dst_ref=got.at[h, me],
                send_sem=send_sems.at[2 * kind + h], recv_sem=sems.at[h, me],
                device_id={"seq": d}, device_id_type=MESH,
            ).start()

        return send

    def send_scale(d):
        pltpu.make_async_remote_copy(
            src_ref=scale_own.at[0:2], dst_ref=scale_got.at[me, 0:2],
            send_sem=send_sems.at[8], recv_sem=scale_sems.at[me],
            device_id={"seq": d}, device_id_type=MESH,
        ).start()

    def but_first(send):
        def guarded(d):
            @pl.when(d != 0)
            def _():
                send(d)

        return guarded

    def await_bytes(ref, sem):
        pltpu.make_async_copy(ref, ref, sem).wait()

    local[0].wait()
    stage(k_rows, k_sent, (0,))

    @pl.when(me == 0)
    def _():
        pl.semaphore_wait(barrier, parts)

    @pl.when(me == 2)
    def _():
        pl.semaphore_wait(barrier, parts - 2)

    @pl.when((me != 0) & (me != 2))
    def _():
        pl.semaphore_wait(barrier, parts - 1)

    send_keys = sender(k_sent, k_got, k_sems, 0, 0)
    to_group(but_first(send_keys))

    @pl.when(me == 0)
    def _():
        signal_group(late_sem)
        pl.semaphore_signal(late_partner_sem, 1, device_id=partner, device_id_type=MESH)

    def inverse_rms(rows):
        def add(c, total):
            part = rows[:, pl.ds(pl.multiple_of(c * 512, 512), 512)].astype(jnp.float32)
            part = part * part
            return total + (
                (part[:, :128] + part[:, 128:256]) + (part[:, 256:384] + part[:, 384:])
            )

        width = rows.shape[1]
        total = lax.fori_loop(0, width // 512, add, jnp.zeros((tok, 128), jnp.float32))
        mean = jnp.sum(jnp.transpose(total), axis=0, keepdims=True) / width
        return lax.rsqrt(mean + EPS)

    scale_own[0:1, :] = inverse_rms(k_rows)
    local[3].wait()
    scale_own[1:2, :] = inverse_rms(q_rows)
    scale_own[2:8, :] = jnp.zeros((6, tok), jnp.float32)
    scale_got[me] = scale_own[...]

    to_group(but_first(send_scale))

    local[1].wait()
    local[2].wait()
    gains[0, 0:2, :] = gain_rows[:, own_cols].astype(jnp.float32)
    gains[0, 2:3, :] = cross_rows[...].astype(jnp.float32)
    gains[0, 3:8, :] = jnp.zeros((5, cols), jnp.float32)
    swap = pltpu.make_async_remote_copy(
        src_ref=gains.at[0], dst_ref=gains.at[1],
        send_sem=send_sems.at[9], recv_sem=gain_sem,
        device_id=partner, device_id_type=MESH,
    )
    fetch = pltpu.make_async_remote_copy(
        src_ref=prompt_ref, dst_ref=tables.at[1],
        send_sem=send_sems.at[10], recv_sem=table_sem,
        device_id=partner, device_id_type=MESH,
    )

    @pl.when(me == 2)
    def _():
        pl.semaphore_wait(late_partner_sem, 1)

    swap.start()
    fetch.start()
    local[4].wait()
    stage(v_rows, v_sent, (0, 1))
    send_values = sender(v_sent, v_got, v_sems, 1, 0)
    to_group(but_first(send_values))
    stage(q_rows, q_sent, (0, 1))
    stage(k_rows, k_sent, (1,))

    @pl.when(me != 0)
    def _():
        pl.semaphore_wait(late_sem, 1)
        send_keys(0)
        send_scale(0)
        send_values(0)

    to_group(sender(q_sent, q_got, q_sems, 2, 0))
    to_group(sender(k_sent, k_got, k_sems, 0, 1))
    to_group(sender(v_sent, v_got, v_sems, 1, 1))
    to_group(sender(q_sent, q_got, q_sems, 2, 1))
    for h in range(2):
        k_got[h, me] = k_sent[h, me]
        v_got[h, me] = v_sent[h, me]
        q_got[h, me] = q_sent[h, me]
    v_wide[:, :, HEAD_DIM:] = jnp.ones((2, parts * tok, HEAD_DIM), jnp.bfloat16)

    swap.wait_recv()

    def from_group(take):
        def chip(c):
            for core in range(2):
                take(source_of(me, c, core))

        over_chips(parts // 2, chip)

    def await_scale(s):
        @pl.when(s != me)
        def _():
            await_bytes(scale_got.at[s, 0:2], scale_sems.at[s])

    from_group(await_scale)
    flipped = jnp.transpose(scale_got[...].reshape(parts * 8, tok))
    for s in range(parts):
        k_scale[s] = jnp.broadcast_to(flipped[:, 8 * s : 8 * s + 1], (tok, 128))
        q_scale[s] = jnp.broadcast_to(flipped[:, 8 * s + 1 : 8 * s + 2], (tok, 128))

    chosen = gains[choice]
    q_gain = chosen[0:1, :] * SCORE_SCALE
    k_gain = chosen[1:2, :]
    cross_gain = chosen[2:3, :] * SCORE_SCALE

    def take_keys(s, h):
        @pl.when(s != me)
        def _():
            await_bytes(k_got.at[h, s], k_sems.at[h, s])

        lanes = slice(h * HEAD_DIM, (h + 1) * HEAD_DIM)
        normed = k_got[h, s].astype(jnp.float32) * k_scale[s] * k_gain[:, lanes]
        k_normed[h, pl.ds(pl.multiple_of(s * tok, tok), tok), :] = normed.astype(jnp.bfloat16)

    def take_values(s, h):
        @pl.when(s != me)
        def _():
            await_bytes(v_got.at[h, s], v_sems.at[h, s])

        v_wide[h, pl.ds(pl.multiple_of(s * tok, tok), tok), :HEAD_DIM] = v_got[h, s]

    def take(h):
        from_group(lambda s: take_keys(s, h))
        from_group(lambda s: take_values(s, h))

    take(0)

    local[5].wait()
    local[6].wait()
    fetch.wait_recv()
    for h in range(2):
        lanes = slice(h * HEAD_DIM, (h + 1) * HEAD_DIM)
        for b in range(2):
            rows = slice(b * 128, (b + 1) * 128)
            cross_keys[h, rows, :] = tables[choice, b * 256 : b * 256 + 128, lanes]
            cross_values[h, rows, :] = tables[choice, b * 256 + 128 : b * 256 + 256, lanes]

    position = lax.broadcasted_iota(jnp.int32, (4 * tok, 128), 1)
    visible = [position < lengths_ref[b] for b in range(2)]
    weight = (GUIDANCE, 1.0 - GUIDANCE)

    def self_scores(blocks, h):
        lanes = slice(h * HEAD_DIM, (h + 1) * HEAD_DIM)
        query = jnp.concatenate(
            [
                (q_got[h, d].astype(jnp.float32) * q_scale[d] * q_gain[:, lanes]).astype(
                    jnp.bfloat16
                )
                for d in blocks
            ],
            axis=0,
        )
        return lax.dot_general(query, k_normed[h], NT, preferred_element_type=jnp.float32)

    def softmax_weights(scores):
        peak = jnp.max(scores, axis=1, keepdims=True)
        return jnp.exp2(scores - peak).astype(jnp.bfloat16)

    def self_values(weights, h):
        sums = jnp.dot(weights, v_wide[h], preferred_element_type=jnp.float32)
        self_out = (sums[:, :HEAD_DIM] / sums[:, HEAD_DIM:]).astype(jnp.bfloat16)
        return self_out.astype(jnp.float32)

    def cross_scores(self_out, h):
        lanes = slice(h * HEAD_DIM, (h + 1) * HEAD_DIM)
        mean = jnp.mean(self_out * self_out, axis=1, keepdims=True)
        query = self_out * lax.rsqrt(mean + EPS) * cross_gain[:, lanes]
        return lax.dot_general(
            query.astype(jnp.bfloat16), cross_keys[h], NT, preferred_element_type=jnp.float32
        )

    def cross_weights(scores):
        shares = []
        for b in range(2):
            branch = jnp.where(visible[b], scores[:, b * 128 : (b + 1) * 128], -jnp.inf)
            branch = jnp.exp2(branch - jnp.max(branch, axis=1, keepdims=True))
            factor = weight[b] / jnp.sum(branch, axis=1, keepdims=True)
            shares.append((branch * factor).astype(jnp.bfloat16))
        return jnp.concatenate(shares, axis=1)

    late_chip = ((ROWS_OF_Y - me // 4) % ROWS_OF_Y) * 2 + (me // 2) % 2
    half = len(CHIPS) // 2
    far = late_chip == CHIPS[half - 1]
    near = functools.reduce(jnp.logical_or, [late_chip == c for c in CHIPS[half:-1]])
    give = jnp.where(far, 0, 1)
    take_up = jnp.where(
        far,
        (source_of(me, CHIPS[half], 0) // 2) * 2,
        (source_of(me, CHIPS[half - 1], 0) // 2) * 2 + 1,
    )

    def put_off(d):
        swapped = jnp.where(d == give, take_up, jnp.where(d == take_up, give, d))
        return jnp.where(far | near, swapped, d)

    def attend(h, *chips):
        blocks = []
        for c in chips:
            first = (source_of(me, c, 0) // 2) * 2
            blocks += [first, first + 1]
        if h == 1:
            blocks = [put_off(d) for d in blocks]
        for d in blocks:

            @pl.when(d != me)
            def _():
                await_bytes(q_got.at[h, d], q_sems.at[h, d])

        halves = [blocks[:4], blocks[4:]]
        scores = [self_scores(half, h) for half in halves]
        weights = [softmax_weights(x) for x in scores]
        self_out = [self_values(x, h) for x in weights]
        scores = [cross_scores(x, h) for x in self_out]
        shares = [cross_weights(x) for x in scores]
        for i, half in enumerate(halves):
            guided = self_out[i] + jnp.dot(
                shares[i], cross_values[h], preferred_element_type=jnp.float32
            )
            guided = guided.astype(jnp.bfloat16)
            for j, d in enumerate(half):
                out_blocks[h, d] = guided[j * tok : (j + 1) * tok]
        lanes = pl.ds(h * HEAD_DIM, HEAD_DIM)

        def send_out(d):
            pltpu.make_async_remote_copy(
                src_ref=out_blocks.at[h, d], dst_ref=out_ref.at[me, :, lanes],
                send_sem=send_sems.at[6 + h], recv_sem=out_sem,
                device_id={"seq": d}, device_id_type=MESH,
            ).start()

        holds_first = functools.reduce(jnp.logical_or, [d == 0 for d in blocks])

        @pl.when(holds_first & (me != 0))
        def _():
            send_out(0)

        for d in blocks:

            @pl.when((d != me) & (d != 0))
            def _():
                send_out(d)

            @pl.when(d == me)
            def _():
                pltpu.make_async_copy(
                    out_blocks.at[h, me], out_ref.at[me, :, lanes], out_sem
                ).start()

    for h in range(2):
        if h == 1:
            take(1)
        over_chips(parts // 2, functools.partial(attend, h), at_once=4)

    swap.wait_send()
    fetch.wait_send()
    some = pl.ds(0, parts - 1)
    for h in range(2):
        await_bytes(k_got.at[h, some], send_sems.at[h])
        await_bytes(v_got.at[h, some], send_sems.at[2 + h])
        await_bytes(q_got.at[h, some], send_sems.at[4 + h])
        await_bytes(out_blocks.at[h, some], send_sems.at[6 + h])
    await_bytes(scale_got.at[some, 0:2], send_sems.at[8])
    await_bytes(out_ref, out_sem)


def arrange(steps_ref, got_ref, out_ref, sems):
    parts, _, cols = got_ref.shape
    choice = choice_of(steps_ref)
    copies = []
    for d in range(parts):
        worker = d + choice * (across(d) - d)
        lanes = slice(d * cols, (d + 1) * cols)
        copies.append(pltpu.make_async_copy(got_ref.at[worker], out_ref.at[:, lanes], sems.at[d]))
    for copy in copies:
        copy.start()
    for copy in copies:
        copy.wait()


def body(q, k, v, timesteps, norm_gain, cross_gain, prompts, lengths):
    parts = lax.axis_size("seq")
    _, tok, width = q.shape
    cols = width // parts
    text = prompts.shape[3]
    bf16, f32 = jnp.bfloat16, jnp.float32
    hbm = pl.BlockSpec(memory_space=pltpu.HBM)
    vmem = pl.BlockSpec(memory_space=pltpu.VMEM)
    smem = pl.BlockSpec(memory_space=pltpu.SMEM)
    dma = pltpu.SemaphoreType.DMA
    blocks = pltpu.VMEM((2, parts, tok, HEAD_DIM), bf16)
    got = pl.pallas_call(
        functools.partial(kernel, (parts, tok, cols)),
        out_shape=pltpu.VMEM((parts, tok, cols), bf16),
        in_specs=[smem] + [hbm] * 7,
        out_specs=vmem,
        scratch_shapes=[
            pltpu.SMEM((2,), jnp.int32),
            pltpu.VMEM((tok, width), bf16),
            pltpu.VMEM((tok, width), bf16),
            pltpu.VMEM((tok, width), bf16),
            pltpu.VMEM((2, width), bf16),
            pltpu.VMEM((1, cols), bf16),
            blocks, blocks, blocks,
            blocks, blocks, blocks,
            pltpu.VMEM((2, parts * tok, HEAD_DIM), bf16),
            pltpu.VMEM((2, parts * tok, 2 * HEAD_DIM), bf16),
            blocks,
            pltpu.VMEM((8, tok), f32),
            pltpu.VMEM((parts, 8, tok), f32),
            pltpu.VMEM((parts, tok, 128), f32),
            pltpu.VMEM((parts, tok, 128), f32),
            pltpu.VMEM((2, 8, cols), f32),
            pltpu.VMEM((2, 4 * text, cols), bf16),
            pltpu.VMEM((2, 2 * text, HEAD_DIM), bf16),
            pltpu.VMEM((2, 2 * text, HEAD_DIM), bf16),
            dma((6,)),
            dma((2, parts)),
            dma((2, parts)),
            dma((2, parts)),
            dma((parts,)),
            dma((11,)),
            dma,
            dma,
            dma,
            dma,
            pltpu.SemaphoreType.REGULAR,
            pltpu.SemaphoreType.REGULAR,
        ],
        compiler_params=pltpu.CompilerParams(
            collective_id=0, has_side_effects=True, vmem_limit_bytes=44 * 2**20
        ),
        name="guided_attention",
    )(
        timesteps,
        *(
            pltpu.with_memory_space_constraint(x, pltpu.HBM)
            for x in (
                lengths,
                q.reshape(tok, width), k.reshape(tok, width), v.reshape(tok, width),
                norm_gain.reshape(2, width), cross_gain, prompts.reshape(4 * text, cols),
            )
        ),
    )
    out = pl.pallas_call(
        arrange,
        out_shape=jax.ShapeDtypeStruct((tok, width), bf16),
        in_specs=[smem, vmem],
        out_specs=hbm,
        scratch_shapes=[dma((parts,))],
        compiler_params=pltpu.CompilerParams(vmem_limit_bytes=8 * 2**20),
        name="arrange",
    )(timesteps, got)
    return out[None]


def solution(mesh):
    placed = (
        P(("expert", "dp"), "seq", None),
        P(("expert", "dp"), "seq", None),
        P(("expert", "dp"), "seq", None),
        P(("expert", "dp")),
        P("expert", None, None),
        P("expert", "seq"),
        P("expert", None, None, None, "seq"),
        P(),
    )
    return jax.shard_map(
        body,
        mesh=mesh,
        in_specs=placed,
        out_specs=P(("expert", "dp"), "seq", None),
        check_vma=False,
    )
```
